128 devices in a mesh: seq: 16 (over y, z), head: 8 (over x, core).
Axes of the slice: x: 4, y: 4, z: 4, core: 2. Of those that a mesh axis runs over, the one named last changes fastest.
Arguments:
- tile_tokens: bfloat16 [16, 8, 16, 128, 1536], P('seq', 'head'), may hold values from -6 to 6
- tile_gain: float32 [2, 1536], replicated, may hold values from 0.1 to 1.9
- tile_wq: bfloat16 [1536, 1536], P(('seq', 'head')), may hold values from -1.1875 to 1.1875
- tile_wkv: bfloat16 [1536, 3072], P(('seq', 'head')), may hold values from -1.1875 to 1.1875
- tile_wo: bfloat16 [1536, 1536], P(('seq', 'head')), may hold values from -0.15625 to 0.15625
- slide_proj: bfloat16 [1536, 768], replicated, may hold values from -0.15625 to 0.15625
- slide_cache: bfloat16 [16384, 768], P('seq'), may hold values from -6 to 6
- slide_gain: float32 [768], replicated, may hold values from 0.1 to 1.9
- slide_qkv: bfloat16 [3, 768, 768], P(None, None, 'head'), may hold values from -1.6875 to 1.6875
- send_map: int32 [8, 16, 16], replicated, may hold values from 0 to 1, as said below
Outputs:
- context: bfloat16 [16384, 768], P('seq', 'head')
- tile_output: bfloat16 [16, 8, 16, 128, 1536], P('seq', 'head')
The draws below stay inside these ranges and needn't reach their ends.
Inputs may be any that keep to these rules, and one draw needn't show every extreme that they name: Entries are 0 or 1. For every h and d exactly 8 sources s have send_map[h, s, d] = 1; for every h some source has a 1 in every column.
All inputs are finite; a program needn't handle non-finite values.
Results may differ from the reference program's by a relative error of at most 0.022.
Values may be sent and summed in bfloat16 or wider, within the bound.
A program may use at most 128 MiB of HBM per device.

```python
import math
import jax
import jax.numpy as jnp
from jax import lax

TILE_WIDTH = 1536
TILE_HEAD_SIZE = 64
TILE_TOKENS = 128
SLIDE_WIDTH = 768
SLIDE_HEAD_SIZE = 48
RATE = 16
SEQ_DEV = 1024
N_SEQ = 16
N_HEAD = 8


def draw_tile_wq(key, part):
    key = jax.random.fold_in(key, 1)
    factor = 1.0 / jnp.sqrt(jnp.float32(TILE_WIDTH))
    own = jnp.clip(jax.random.normal(key, (TILE_WIDTH, TILE_WIDTH), jnp.float32), -6.0, 6.0)
    return jnp.clip(own * factor, -1.1875, 1.1875).astype(jnp.bfloat16)


def draw_tile_wkv(key, part):
    key = jax.random.fold_in(key, 2)
    factor = 1.0 / jnp.sqrt(jnp.float32(TILE_WIDTH))
    own = jnp.clip(jax.random.normal(key, (TILE_WIDTH, 2 * TILE_WIDTH), jnp.float32), -6.0, 6.0)
    return jnp.clip(own * factor, -1.1875, 1.1875).astype(jnp.bfloat16)


def draw_slide_qkv(key, part):
    key = jax.random.fold_in(key, 4)
    factor = 1.0 / jnp.sqrt(jnp.float32(SLIDE_WIDTH))
    own = jnp.clip(jax.random.normal(key, (3, SLIDE_WIDTH, SLIDE_WIDTH), jnp.float32), -6.0, 6.0)
    return jnp.clip(own * factor, -1.6875, 1.6875).astype(jnp.bfloat16)


def draw_tile_tokens(key, part):
    key = jax.random.fold_in(key, 3)
    shape = (N_SEQ, N_HEAD, N_SEQ, TILE_TOKENS, TILE_WIDTH)
    return jnp.clip(jax.random.normal(key, shape, jnp.float32), -6.0, 6.0).astype(jnp.bfloat16)


def draw_slide_cache(key, part):
    key = jax.random.fold_in(key, 5)
    rows = N_SEQ * SEQ_DEV
    return jnp.clip(jax.random.normal(key, (rows, SLIDE_WIDTH), jnp.float32), -6.0, 6.0).astype(jnp.bfloat16)


def draw_send_map(key, part):
    key = jax.random.fold_in(key, 7)
    seq_count = N_SEQ
    groups = N_HEAD
    first_key, second_key = jax.random.split(key)
    ranking = jax.vmap(lambda k: jax.random.permutation(k, seq_count))(jax.random.split(first_key, groups))
    shuffled = jax.vmap(lambda k: jax.random.permutation(k, seq_count))(jax.random.split(second_key, groups * seq_count))
    shuffled = shuffled.reshape(groups, seq_count, seq_count)
    sources = jnp.arange(seq_count, dtype=jnp.int32)
    scores = (ranking[:, None, :] * (seq_count // 2) + shuffled) * seq_count + sources[None, None, :]
    unused, chosen = lax.top_k(scores, seq_count // 2)
    marks = jnp.sum((chosen[:, :, :, None] == sources[None, None, None, :]).astype(jnp.int32), axis=2)
    return jnp.transpose(marks, (0, 2, 1)).astype(jnp.int32)


def block_levels(key, extent, cuts, low, high):
    level, own = 1.0, jax.random.fold_in(key, 6)
    for position, shards_of in cuts:
        steps = jnp.exp(jax.random.uniform(jax.random.fold_in(own, position), (shards_of,), jnp.float32, low / len(cuts), high / len(cuts)))
        level = level * jnp.repeat(steps, extent[position] // shards_of).reshape([-1 if axis == position else 1 for axis in range(len(extent))])
    return level


def bell_draw(key, dims, deviation, reach, cuts=(), held_as=jnp.bfloat16):
    loudness = block_levels(key, dims, cuts, -0.22, 0.18) if cuts else 1.0
    entries = jax.random.normal(key, dims, jnp.float32) * deviation * loudness
    return jnp.minimum(jnp.maximum(entries, -reach), reach).astype(held_as)


def setup_inputs(seed: int = 0) -> dict:
    key_list = jax.random.split(jax.random.key(seed), 11)
    return {
        "tile_tokens": draw_tile_tokens(jax.random.fold_in(key_list[10], 71), 0),
        "tile_gain": jnp.clip(1.0 + 0.18 * jax.random.normal(key_list[1], (2, TILE_WIDTH), jnp.float32), 0.1, 1.9),
        "tile_wq": draw_tile_wq(jax.random.fold_in(key_list[10], 71), 0),
        "tile_wkv": draw_tile_wkv(jax.random.fold_in(key_list[10], 71), 0),
        "tile_wo": bell_draw(key_list[4], (TILE_WIDTH, TILE_WIDTH), TILE_WIDTH ** -0.5, 0.15625, ((0, 128),)),
        "slide_proj": bell_draw(key_list[5], (TILE_WIDTH, SLIDE_WIDTH), TILE_WIDTH ** -0.5, 0.15625),
        "slide_cache": draw_slide_cache(jax.random.fold_in(key_list[10], 71), 0),
        "slide_gain": jnp.clip(1.0 + 0.18 * jax.random.normal(key_list[7], (SLIDE_WIDTH,), jnp.float32), 0.1, 1.9),
        "slide_qkv": draw_slide_qkv(jax.random.fold_in(key_list[10], 71), 0),
        "send_map": draw_send_map(jax.random.fold_in(key_list[10], 71), 0),
    }


EPS = 1e-05

def stored(values):
    return lax.optimization_barrier(values.astype(jnp.bfloat16))

def norm_rows(values, gain):
    values = values.astype(jnp.float32)
    center = values - lax.optimization_barrier(jnp.mean(values, axis=-1, keepdims=True))
    spread = lax.optimization_barrier(jnp.mean(center * center, axis=-1, keepdims=True))
    return center * lax.rsqrt(spread + EPS) * gain

def encode_tiles(tile_block, tile_gain, w_query, w_pairs, w_out):
    length = tile_block.shape[1]
    features = tile_block.shape[2]
    head_count = features // TILE_HEAD_SIZE
    score_scale = 1.0 / math.sqrt(TILE_HEAD_SIZE)

    def one_tile(tile):
        normed = stored(norm_rows(tile, tile_gain[0]))
        key_value = stored(jnp.dot(normed, w_pairs, preferred_element_type=jnp.float32))
        query_rows = stored(jnp.dot(normed, w_query, preferred_element_type=jnp.float32))
        query_rows = query_rows.reshape(length, head_count, TILE_HEAD_SIZE).astype(jnp.float32)
        key_rows = key_value[:, :features].reshape(length, head_count, TILE_HEAD_SIZE).astype(jnp.float32)
        value_rows = key_value[:, features:].reshape(length, head_count, TILE_HEAD_SIZE).astype(jnp.float32)
        scores = jnp.einsum('qhd,khd->hqk', query_rows, key_rows) * score_scale
        highest = lax.optimization_barrier(jnp.max(scores, axis=2, keepdims=True))
        weights = jnp.exp(scores - highest)
        attention = stored(weights / lax.optimization_barrier(jnp.sum(weights, axis=2, keepdims=True))).astype(jnp.float32)
        context = stored(jnp.einsum('hqk,khd->qhd', attention, value_rows)).reshape(length, features)
        layer = stored(tile.astype(jnp.float32) + jnp.dot(context, w_out, preferred_element_type=jnp.float32))
        embedded = stored(norm_rows(layer[0], tile_gain[1]))
        return (layer, embedded)
    return lax.map(one_tile, tile_block)

def partial_softmax(query_rows, key_rows, value_rows, score_scale):
    rows = query_rows.shape[0]
    block = min(512, rows)
    grouped = query_rows.reshape(rows // block, block, query_rows.shape[1], query_rows.shape[2]).astype(jnp.float32)
    key_float = key_rows.astype(jnp.float32)
    value_float = value_rows.astype(jnp.float32)

    def one_block(block_rows):
        scores = jnp.einsum('qhe,khe->hqk', block_rows, key_float) * score_scale
        highest = lax.optimization_barrier(jnp.max(scores, axis=2))
        weights = jnp.exp(scores - highest[:, :, None])
        totals = lax.optimization_barrier(jnp.sum(weights, axis=2))
        rounded = stored(weights).astype(jnp.float32)
        numer = jnp.einsum('hqk,khe->hqe', rounded, value_float)
        return (highest, totals, numer)
    highest, totals, numer = lax.map(one_block, grouped)
    heads_here = query_rows.shape[1]
    highest = jnp.transpose(highest, (1, 0, 2)).reshape(heads_here, rows)
    totals = jnp.transpose(totals, (1, 0, 2)).reshape(heads_here, rows)
    numer = jnp.transpose(numer, (1, 0, 2, 3)).reshape(heads_here, rows, query_rows.shape[2])
    return (highest, totals, numer)

def combine_levels(near, far, offsets):
    near_top, near_total, near_numer = near
    far_top, far_total, far_numer = far
    rows = near_top.shape[1]
    phase = jnp.arange(rows, dtype=jnp.int32) % RATE
    picked = phase[None, :] == offsets[:, None]
    far_top_rows = jnp.repeat(far_top, RATE, axis=1)
    far_total_rows = jnp.repeat(far_total, RATE, axis=1)
    far_numer_rows = jnp.repeat(far_numer, RATE, axis=1)
    highest = jnp.where(picked, jnp.maximum(near_top, far_top_rows), near_top)
    near_factor = jnp.exp(near_top - highest)
    far_factor = jnp.where(picked, jnp.exp(jnp.minimum(far_top_rows - highest, 0.0)), 0.0)
    numer = near_numer * near_factor[:, :, None] + far_numer_rows * far_factor[:, :, None]
    totals = near_total * near_factor + far_total_rows * far_factor
    return numer / totals[:, :, None]

def reference(tile_tokens, tile_gain, tile_wq, tile_wkv, tile_wo, slide_proj, slide_cache, slide_gain, slide_qkv, send_map):
    groups = send_map.shape[0]
    seq_count = send_map.shape[1]
    held_count = seq_count // 2
    slide_width = slide_proj.shape[1]
    incoming = jnp.transpose(send_map, (0, 2, 1))
    arrived = jnp.cumsum(incoming, axis=2)
    ranks = jnp.arange(held_count, dtype=jnp.int32)
    source = lax.optimization_barrier(jnp.sum((arrived[:, :, None, :] <= ranks[None, None, :, None]).astype(jnp.int32), axis=3))
    before = jnp.transpose(jnp.cumsum(send_map, axis=2) - send_map, (0, 2, 1))
    slot_index = jnp.take_along_axis(before, source, axis=2).astype(jnp.int32)
    group_index = jnp.broadcast_to(jnp.arange(groups, dtype=jnp.int32)[:, None, None], source.shape)

    def encode_group(indices):
        source_rows, slot_rows, group_rows = indices
        chosen = tile_tokens[source_rows, group_rows, slot_rows]
        layers, embedded = encode_tiles(chosen, tile_gain, tile_wq, tile_wkv, tile_wo)
        fresh_rows = jnp.dot(embedded, slide_proj, preferred_element_type=jnp.float32).astype(jnp.bfloat16)
        return (layers, fresh_rows)
    layers, fresh = lax.map(encode_group, (source.reshape(-1, held_count), slot_index.reshape(-1, held_count), group_index.reshape(-1, held_count)))
    tile_length = tile_tokens.shape[3]
    tile_features = tile_tokens.shape[4]
    tile_table = jnp.zeros(tile_tokens.shape, jnp.bfloat16)
    tile_table = tile_table.at[source.reshape(-1), group_index.reshape(-1), slot_index.reshape(-1)].set(layers.reshape(-1, tile_length, tile_features))
    table = jnp.zeros((seq_count, groups, seq_count, slide_width), jnp.bfloat16)
    table = table.at[source.reshape(-1), group_index.reshape(-1), slot_index.reshape(-1)].set(fresh.reshape(-1, slide_width))
    live_count = lax.optimization_barrier(jnp.sum(send_map, axis=2))
    places = jnp.arange(seq_count, dtype=jnp.int32)
    live = places[None, None, :] < jnp.transpose(live_count, (1, 0))[:, :, None]
    shards = slide_cache.reshape(seq_count, SEQ_DEV, slide_width)
    span = groups * seq_count
    head_part = shards[:, :span].reshape(seq_count, groups, seq_count, slide_width)
    head_part = jnp.where(live[:, :, :, None], table, head_part).reshape(seq_count, span, slide_width)
    slide_input = jnp.concatenate([head_part, shards[:, span:]], axis=1)
    total_len = seq_count * SEQ_DEV
    normed = stored(norm_rows(slide_input.reshape(total_len, slide_width), slide_gain))
    projected = [stored(jnp.dot(normed, slide_qkv[c], preferred_element_type=jnp.float32)) for c in range(3)]
    head_total = slide_width // SLIDE_HEAD_SIZE
    score_scale = 1.0 / math.sqrt(SLIDE_HEAD_SIZE)

    def per_head(head_id):
        pieces = [lax.dynamic_slice_in_dim(p, head_id * SLIDE_HEAD_SIZE, SLIDE_HEAD_SIZE, 1).reshape(total_len, 1, SLIDE_HEAD_SIZE) for p in projected]
        segments = [p.reshape(seq_count, SEQ_DEV, 1, SLIDE_HEAD_SIZE) for p in pieces]
        near = lax.map(lambda seg: partial_softmax(seg[0], seg[1], seg[2], score_scale), tuple(segments))
        near_top = jnp.transpose(near[0], (1, 0, 2)).reshape(1, total_len)
        near_total = jnp.transpose(near[1], (1, 0, 2)).reshape(1, total_len)
        near_numer = jnp.transpose(near[2], (1, 0, 2, 3)).reshape(1, total_len, SLIDE_HEAD_SIZE)
        offset = (head_id % RATE).astype(jnp.int32)
        sparse = [lax.dynamic_index_in_dim(p.reshape(total_len // RATE, RATE, 1, SLIDE_HEAD_SIZE), offset, 1, keepdims=False) for p in pieces]
        far = partial_softmax(sparse[0], sparse[1], sparse[2], score_scale)
        merged = combine_levels((near_top, near_total, near_numer), far, jnp.reshape(offset, (1,)))
        return merged[0]
    outputs = lax.map(per_head, jnp.arange(head_total, dtype=jnp.int32))
    context = jnp.transpose(outputs, (1, 0, 2)).reshape(total_len, slide_width).astype(jnp.bfloat16)
    return (context, tile_table)
```

```python
import functools
import math

import jax
import jax.numpy as jnp
from jax import lax
from jax.experimental import pallas as pl
from jax.experimental.pallas import tpu as pltpu
from jax.sharding import PartitionSpec as P

TILE_HEAD_SIZE = 64
SLIDE_HEAD_SIZE = 48
RATE = 16
EPS = 1e-05
GROUP = 4
COLS = 512


def norm_rows(values, gain):
    values = values.astype(jnp.float32)
    center = values - jnp.mean(values, axis=-1, keepdims=True)
    spread = jnp.mean(center * center, axis=-1, keepdims=True)
    return center * lax.rsqrt(spread + EPS) * gain


def tile_kernel(live_ref, x_ref, gain_ref, wq_ref, wkv_ref, wo_ref, out_ref, emb_ref, xn, q, kv, ctx):
    step = pl.program_id(0)
    live = live_ref[0]
    tiles, length, width = x_ref.shape
    rows = tiles * length

    @pl.when(step * tiles < live)
    def _():
        for t in range(tiles):

            def norm(r, _):
                at = pl.ds(pl.multiple_of(r * 32, 32), 32)
                values = norm_rows(x_ref[t, at, :], gain_ref[0:1, :])
                xn[pl.ds(pl.multiple_of(t * length + r * 32, 32), 32), :] = values.astype(jnp.bfloat16)
                return 0

            lax.fori_loop(0, length // 32, norm, 0)

        def project(n, _):
            at = pl.ds(pl.multiple_of(n * COLS, COLS), COLS)
            q[:, at] = jnp.dot(xn[...], wq_ref[:, at], preferred_element_type=jnp.float32).astype(jnp.bfloat16)
            return 0

        lax.fori_loop(0, width // COLS, project, 0)

        def project_kv(n, _):
            at = pl.ds(pl.multiple_of(n * COLS, COLS), COLS)
            kv[:, at] = jnp.dot(xn[...], wkv_ref[:, at], preferred_element_type=jnp.float32).astype(jnp.bfloat16)
            return 0

        lax.fori_loop(0, 2 * width // COLS, project_kv, 0)

        lane = lax.broadcasted_iota(jnp.int32, (length, 128), 1)
        first = lane < TILE_HEAD_SIZE
        ones_a = jnp.where(first, 1.0, 0.0).astype(jnp.bfloat16)
        ones_b = jnp.where(first, 0.0, 1.0).astype(jnp.bfloat16)
        ones = jnp.concatenate([ones_a, ones_b], axis=0)
        scale = 1.0 / math.sqrt(TILE_HEAD_SIZE)

        def attend(p, _):
            at = pl.ds(pl.multiple_of(p * 128, 128), 128)
            vat = pl.ds(pl.multiple_of(width + p * 128, 128), 128)
            for t in range(tiles):
                tat = slice(t * length, (t + 1) * length)
                qp, kp, vp = q[tat, at], kv[tat, at], kv[tat, vat]
                keys = jnp.concatenate([kp * ones_a, kp * ones_b], axis=0)
                vals = jnp.concatenate([vp * ones_a, vp * ones_b], axis=0)
                vals = jnp.concatenate([vals, ones], axis=1)
                s = lax.dot_general(
                    qp, keys, (((1,), (1,)), ((), ())), preferred_element_type=jnp.float32
                )
                parts = []
                for half in range(2):
                    sh = s[:, half * length : (half + 1) * length]
                    top = jnp.max(sh, axis=1, keepdims=True)
                    parts.append(jnp.exp((sh - top) * scale).astype(jnp.bfloat16))
                w = jnp.concatenate(parts, axis=1)
                o = jnp.dot(w, vals, preferred_element_type=jnp.float32)
                ctx[tat, at] = (o[:, :128] / o[:, 128:]).astype(jnp.bfloat16)
            return 0

        lax.fori_loop(0, width // 128, attend, 0)

        def project_out(n, _):
            at = pl.ds(pl.multiple_of(n * COLS, COLS), COLS)
            y = jnp.dot(ctx[...], wo_ref[:, at], preferred_element_type=jnp.float32)
            for t in range(tiles):
                xt = x_ref[t, :, at].astype(jnp.float32)
                yt = xt + y[t * length : (t + 1) * length]
                out_ref[t, :, at] = jnp.where(step * tiles + t < live, yt, 0.0).astype(jnp.bfloat16)
            return 0

        lax.fori_loop(0, width // COLS, project_out, 0)
        for t in range(tiles):
            emb_ref[t] = norm_rows(out_ref[t, 0:16, :], gain_ref[1:2, :])[0:1]

    @pl.when(step * tiles >= live)
    def _():
        out_ref[...] = jnp.zeros_like(out_ref)
        emb_ref[...] = jnp.zeros_like(emb_ref)


def encode_tiles(live, tiles, gain, wq, wkv, wo):
    slots, length, width = tiles.shape
    rows = GROUP * length
    whole = pl.BlockSpec(memory_space=pltpu.VMEM)
    return pl.pallas_call(
        tile_kernel,
        grid_spec=pltpu.PrefetchScalarGridSpec(
            num_scalar_prefetch=1,
            grid=(slots // GROUP,),
            in_specs=[
                pl.BlockSpec((GROUP, length, width), lambda i, live: (i, 0, 0)),
                whole,
                whole,
                whole,
                whole,
            ],
            out_specs=[
                pl.BlockSpec((GROUP, length, width), lambda i, live: (i, 0, 0)),
                pl.BlockSpec((GROUP, 1, width), lambda i, live: (i, 0, 0)),
            ],
            scratch_shapes=[
                pltpu.VMEM((rows, width), jnp.bfloat16),
                pltpu.VMEM((rows, width), jnp.bfloat16),
                pltpu.VMEM((rows, 2 * width), jnp.bfloat16),
                pltpu.VMEM((rows, width), jnp.bfloat16),
            ],
        ),
        out_shape=[
            jax.ShapeDtypeStruct((slots, length, width), jnp.bfloat16),
            jax.ShapeDtypeStruct((slots, 1, width), jnp.float32),
        ],
        compiler_params=pltpu.CompilerParams(vmem_limit_bytes=56 * 1024 * 1024),
        name="tile_layer",
    )(live, tiles, gain, wq, wkv, wo)


def partial_softmax(query_rows, key_rows, value_rows, score_scale):
    rows = query_rows.shape[0]
    block = min(512, rows)
    grouped = query_rows.reshape(rows // block, block, query_rows.shape[1], query_rows.shape[2])

    def one_block(block_rows):
        scores = (
            jnp.einsum("qhe,khe->hqk", block_rows, key_rows, preferred_element_type=jnp.float32)
            * score_scale
        )
        highest = jnp.max(scores, axis=2)
        weights = jnp.exp(scores - highest[:, :, None])
        totals = jnp.sum(weights, axis=2)
        numer = jnp.einsum(
            "hqk,khe->hqe",
            weights.astype(jnp.bfloat16),
            value_rows,
            preferred_element_type=jnp.float32,
        )
        return (highest, totals, numer)

    highest, totals, numer = lax.map(one_block, grouped)
    heads_here = query_rows.shape[1]
    highest = jnp.transpose(highest, (1, 0, 2)).reshape(heads_here, rows)
    totals = jnp.transpose(totals, (1, 0, 2)).reshape(heads_here, rows)
    numer = jnp.transpose(numer, (1, 0, 2, 3)).reshape(heads_here, rows, query_rows.shape[2])
    return (highest, totals, numer)


def combine_levels(near, far, offsets):
    near_top, near_total, near_numer = near
    far_top, far_total, far_numer = far
    rows = near_top.shape[1]
    phase = jnp.arange(rows, dtype=jnp.int32) % RATE
    picked = phase[None, :] == offsets[:, None]
    far_top_rows = jnp.repeat(far_top, RATE, axis=1)
    far_total_rows = jnp.repeat(far_total, RATE, axis=1)
    far_numer_rows = jnp.repeat(far_numer, RATE, axis=1)
    highest = jnp.where(picked, jnp.maximum(near_top, far_top_rows), near_top)
    near_factor = jnp.exp(near_top - highest)
    far_factor = jnp.where(picked, jnp.exp(jnp.minimum(far_top_rows - highest, 0.0)), 0.0)
    numer = near_numer * near_factor[:, :, None] + far_numer_rows * far_factor[:, :, None]
    totals = near_total * near_factor + far_total_rows * far_factor
    return numer / totals[:, :, None]


def per_device(
    tile_tokens,
    tile_gain,
    tile_wq,
    tile_wkv,
    tile_wo,
    slide_proj,
    slide_cache,
    slide_gain,
    slide_qkv,
    send_map,
):
    local_tiles = tile_tokens[0, 0]
    slot_count = local_tiles.shape[0]
    seq_index = lax.axis_index("seq")
    head_index = lax.axis_index("head")
    w_query, w_pairs, w_out = (
        lax.all_gather(tile_wq, ("seq", "head"), axis=0, tiled=True),
        lax.all_gather(tile_wkv, ("seq", "head"), axis=0, tiled=True),
        lax.all_gather(tile_wo, ("seq", "head"), axis=0, tiled=True),
    )
    row_plan = lax.dynamic_index_in_dim(send_map, seq_index, 1, keepdims=False)
    live_count = jnp.sum(row_plan, axis=1)
    own_live = lax.dynamic_slice_in_dim(live_count, head_index, 1, 0)
    tile_layers, embedded = encode_tiles(own_live, local_tiles, tile_gain, w_query, w_pairs, w_out)
    slot_rows = embedded[:, 0].astype(jnp.bfloat16)
    fresh = jnp.dot(slot_rows, slide_proj, preferred_element_type=jnp.float32).astype(jnp.bfloat16)
    shared = lax.all_gather(fresh[None], "head", axis=0, tiled=True)
    groups = shared.shape[0]
    slide_width = shared.shape[2]
    span = groups * slot_count
    places = jnp.arange(slot_count, dtype=jnp.int32)
    live = (places[None, :] < live_count[:, None]).reshape(span)
    head_part = jnp.where(live[:, None], shared.reshape(span, slide_width), slide_cache[:span])
    slide_input = jnp.concatenate([head_part, slide_cache[span:]], axis=0)
    seq_rows = slide_input.shape[0]
    normed = norm_rows(slide_input, slide_gain).astype(jnp.bfloat16)
    projected = jnp.einsum(
        "tf,cfe->cte", normed, slide_qkv, preferred_element_type=jnp.float32
    ).astype(jnp.bfloat16)
    heads_here = slide_qkv.shape[2] // SLIDE_HEAD_SIZE
    query_rows = projected[0].reshape(seq_rows, heads_here, SLIDE_HEAD_SIZE)
    key_rows = projected[1].reshape(seq_rows, heads_here, SLIDE_HEAD_SIZE)
    value_rows = projected[2].reshape(seq_rows, heads_here, SLIDE_HEAD_SIZE)
    score_scale = 1.0 / math.sqrt(SLIDE_HEAD_SIZE)
    near = partial_softmax(query_rows, key_rows, value_rows, score_scale)
    offsets = (head_index * heads_here + jnp.arange(heads_here, dtype=jnp.int32)) % RATE
    selector = (offsets[:, None] == jnp.arange(RATE, dtype=jnp.int32)[None, :]).astype(jnp.bfloat16)

    def thin_rows(values):
        grouped = values.reshape(seq_rows // RATE, RATE, heads_here, SLIDE_HEAD_SIZE)
        return jnp.einsum(
            "rphe,hp->rhe", grouped, selector, preferred_element_type=jnp.float32
        ).astype(jnp.bfloat16)

    sparse_query = thin_rows(query_rows)
    both = jnp.concatenate([thin_rows(key_rows), thin_rows(value_rows)], axis=2)
    both = lax.all_gather(both, "seq", axis=0, tiled=True)
    far = partial_softmax(
        sparse_query, both[:, :, :SLIDE_HEAD_SIZE], both[:, :, SLIDE_HEAD_SIZE:], score_scale
    )
    merged = combine_levels(near, far, offsets)
    context = (
        jnp.transpose(merged, (1, 0, 2))
        .reshape(seq_rows, heads_here * SLIDE_HEAD_SIZE)
        .astype(jnp.bfloat16)
    )
    return (context, tile_layers[None, None])


def solution(mesh):
    return jax.shard_map(
        per_device,
        mesh=mesh,
        in_specs=(
            P("seq", "head", None, None, None),
            P(),
            P(("seq", "head"), None),
            P(("seq", "head"), None),
            P(("seq", "head"), None),
            P(),
            P("seq", None),
            P(),
            P(None, None, "head"),
            P(),
        ),
        out_specs=(P("seq", "head"), P("seq", "head", None, None, None)),
        check_vma=False,
    )
```

```python
import math

import jax
import jax.numpy as jnp
from jax import lax
from jax.experimental import pallas as pl
from jax.experimental.pallas import tpu as pltpu
from jax.sharding import PartitionSpec as P

TILE_HEAD_SIZE = 64
SLIDE_HEAD_SIZE = 48
RATE = 16
EPS = 1e-05
GROUP = 4
COLS = 512
MESH = pl.DeviceIdType.MESH
ORDERS = (("x", "y", "z"), ("y", "z", "x"), ("z", "x", "y"))
RING = 4


class Place:
    def __init__(self):
        seq, head = lax.axis_index("seq"), lax.axis_index("head")
        self.core = head % 2
        self.at = {"x": head // 2, "y": seq // RING, "z": seq % RING}

    def device(self, axis=None, shift=0, core=None):
        at = dict(self.at)
        if axis is not None:
            at[axis] = (at[axis] + shift) % RING
        core = self.core if core is None else core
        return (at["y"] * RING + at["z"], at["x"] * 2 + core)

    def index(self, matrix, core, part, phase, shift):
        order = ORDERS[part]
        at = {}
        for number, axis in enumerate(order):
            if number < phase:
                at[axis] = None
            elif number == phase:
                at[axis] = (self.at[axis] + shift) % RING
            else:
                at[axis] = self.at[axis]
        every = slice(None)
        x, y, z = at["x"], at["y"], at["z"]
        low, high = (every, every) if x is None else (x % 2, x // 2)
        return (
            matrix,
            low,
            core,
            part,
            every if y is None else y,
            every if z is None else z,
            high,
        )


def gather_kernel(w_ref, full, inbox, own, swap_send, swap_recv, send, recv, pair_send, pair_recv, keep):
    here = Place()
    core, other = here.core, 1 - here.core
    x = here.at["x"]
    low = x % 2
    mate = x + 1 - 2 * low
    spot = here.device()[0]
    members = [(spot, x * 2 + other), (spot, mate * 2 + core), (spot, mate * 2 + other)]
    me = 2 * low + core
    ids = [2 * low + other, 2 * (1 - low) + core, 2 * (1 - low) + other]

    barrier = pltpu.get_barrier_semaphore()
    partners = [here.device(a, s) for a in "xyz" for s in (1, 3)] + [members[0], members[2]]
    for partner in partners:
        pl.semaphore_signal(barrier, inc=1, device_id=partner, device_id_type=MESH)
    pl.semaphore_wait(barrier, len(partners))

    swaps = []
    for n in range(3):
        swaps.append(
            pltpu.make_async_remote_copy(
                src_ref=w_ref.at[ids[n]],
                dst_ref=inbox.at[n],
                send_sem=swap_send.at[n],
                recv_sem=swap_recv.at[n],
                device_id=members[n],
                device_id_type=MESH,
            )
        )
        swaps[n].start()
    for n in range(3):
        swaps[n].wait_recv()
    count = 4 * 48
    row = lax.broadcasted_iota(jnp.int32, (count, count), 0)
    col = lax.broadcasted_iota(jnp.int32, (count, count), 1)
    matrix, member, inner = row // 48, (row % 48) // 12, row % 12
    total = None
    sources = [w_ref[me]] + [inbox[n] for n in range(3)]
    names = [me] + ids
    for piece, name in zip(sources, names):
        want = matrix * 12 + inner
        pick = jnp.where((member == name) & (want == col), 1.0, 0.0).astype(jnp.bfloat16)[:, :48]
        term = jnp.dot(pick, piece, preferred_element_type=jnp.float32)
        total = term if total is None else total + term
    for m in range(4):
        for p in range(3):
            own[m, p] = total[m * 48 : (m + 1) * 48, p * 128 : (p + 1) * 128].astype(jnp.bfloat16)

    def move(m, p, phase, piece, origin, target):
        spots = here.index(m, core, p, phase, origin)
        axis = ORDERS[p][phase]
        src = own.at[m, p] if phase == 0 and origin == 0 else full.at[spots]
        return pltpu.make_async_remote_copy(
            src_ref=src,
            dst_ref=full.at[spots],
            send_sem=send.at[m, p, phase, piece],
            recv_sem=recv.at[m, p, phase, piece],
            device_id=here.device(axis, target),
            device_id_type=MESH,
        )

    def arrive(m, p, phase, piece, origin):
        spots = here.index(m, core, p, phase, origin)
        axis = ORDERS[p][phase]
        pltpu.make_async_remote_copy(
            src_ref=full.at[spots],
            dst_ref=full.at[spots],
            send_sem=send.at[m, p, phase, piece],
            recv_sem=recv.at[m, p, phase, piece],
            device_id=here.device(axis, 1),
            device_id_type=MESH,
        ).wait_recv()

    def pair(m, p, piece, phase, origin, side):
        spots = here.index(m, side, p, phase, origin)
        return pltpu.make_async_remote_copy(
            src_ref=full.at[spots],
            dst_ref=full.at[spots],
            send_sem=pair_send.at[m, p, piece],
            recv_sem=pair_recv.at[m, p, piece],
            device_id=members[0],
            device_id_type=MESH,
        )

    sent = []

    def go(copy):
        copy.start()
        sent.append(copy)

    todo = [(m, p) for m in range(4) for p in range(3)]
    keeps = []
    for m, p in todo:
        go(move(m, p, 0, 0, 0, 1))
        go(move(m, p, 0, 1, 0, 3))
    for m, p in todo:
        copy = pltpu.make_async_copy(own.at[m, p], full.at[here.index(m, core, p, 0, 0)], keep.at[m, p])
        copy.start()
        keeps.append(copy)
    for copy in keeps:
        copy.wait()
    for phase in range(3):
        for m, p in todo:
            arrive(m, p, phase, 0, 3)
            arrive(m, p, phase, 1, 1)
            if m % 2 == 0:
                go(move(m, p, phase, 2, 3, 1))
            else:
                go(move(m, p, phase, 2, 1, 3))
            if phase == 2:
                go(pair(m, p, 1, 2, 3, core))
                go(pair(m, p, 2, 2, 1, core))
        for m, p in todo:
            arrive(m, p, phase, 2, 2)
            if phase < 2:
                go(move(m, p, phase + 1, 0, 0, 1))
                go(move(m, p, phase + 1, 1, 0, 3))
            if phase == 1:
                go(pair(m, p, 0, 2, 0, core))
            if phase == 2:
                go(pair(m, p, 3, 2, 2, core))
    for m, p in todo:
        for piece, origin in enumerate((0, 3, 1, 2)):
            pair(m, p, piece, 2, origin, other).wait_recv()
    for copy in swaps + sent:
        copy.wait_send()


def gather_weights(wq, wkv, wo):
    rows, width = wq.shape
    parts = jnp.concatenate([wkv, wq, wo], axis=1)
    parts = parts.reshape(rows, 4, 4, width // 4)
    parts = jnp.transpose(parts, (2, 1, 0, 3)).reshape(4, 4 * rows, width // 4)
    dma = pltpu.SemaphoreType.DMA
    return pl.pallas_call(
        gather_kernel,
        in_specs=[pl.BlockSpec(memory_space=pltpu.VMEM)],
        out_specs=pl.BlockSpec(memory_space=pl.ANY),
        out_shape=jax.ShapeDtypeStruct((4, 2, 2, 3, 4, 4, 2, 48, 128), jnp.bfloat16),
        scratch_shapes=[
            pltpu.VMEM((3, 48, 384), jnp.bfloat16),
            pltpu.VMEM((4, 3, 48, 128), jnp.bfloat16),
            dma((3,)),
            dma((3,)),
            dma((4, 3, 3, 3)),
            dma((4, 3, 3, 3)),
            dma((4, 3, 4)),
            dma((4, 3, 4)),
            dma((4, 3)),
        ],
        compiler_params=pltpu.CompilerParams(collective_id=0, has_side_effects=True, vmem_limit_bytes=40 * 1024 * 1024),
        name="weight_gather",
    )(parts)


def norm_rows(values, gain):
    values = values.astype(jnp.float32)
    center = values - jnp.mean(values, axis=-1, keepdims=True)
    spread = jnp.mean(center * center, axis=-1, keepdims=True)
    return center * lax.rsqrt(spread + EPS) * gain


def tile_kernel(live_ref, x_ref, gain_ref, w_ref, out_ref, emb_ref, w, xn, q, kv, ctx, load):
    step = pl.program_id(0)
    live = live_ref[0]
    tiles, length, width = x_ref.shape
    blocks = COLS // 128
    loads = [pltpu.make_async_copy(w_ref.at[m], w.at[m], load.at[m]) for m in range(4)]

    @pl.when(step == 0)
    def _():
        for copy in loads:
            copy.start()

    def ready(m):
        @pl.when(step == 0)
        def _():
            loads[m].wait()

    def columns(m, n):
        return jnp.concatenate([w[m, n * blocks + j] for j in range(blocks)], axis=1)

    @pl.when(step * tiles < live)
    def _():
        for t in range(tiles):

            def norm(r, _):
                at = pl.ds(pl.multiple_of(r * 32, 32), 32)
                values = norm_rows(x_ref[t, at, :], gain_ref[0:1, :])
                xn[pl.ds(pl.multiple_of(t * length + r * 32, 32), 32), :] = values.astype(jnp.bfloat16)
                return 0

            lax.fori_loop(0, length // 32, norm, 0)

        for m, ref, base in ((0, kv, 0), (1, kv, width), (2, q, 0)):
            ready(m)

            def project(n, _):
                at = pl.ds(pl.multiple_of(base + n * COLS, COLS), COLS)
                ref[:, at] = jnp.dot(
                    xn[...], columns(m, n), preferred_element_type=jnp.float32
                ).astype(jnp.bfloat16)
                return 0

            lax.fori_loop(0, width // COLS, project, 0)

        lane = lax.broadcasted_iota(jnp.int32, (length, 128), 1)
        first = lane < TILE_HEAD_SIZE
        ones_a = jnp.where(first, 1.0, 0.0).astype(jnp.bfloat16)
        ones_b = jnp.where(first, 0.0, 1.0).astype(jnp.bfloat16)
        ones = jnp.concatenate([ones_a, ones_b], axis=0)
        scale = 1.0 / math.sqrt(TILE_HEAD_SIZE)

        def attend(p, _):
            at = pl.ds(pl.multiple_of(p * 128, 128), 128)
            vat = pl.ds(pl.multiple_of(width + p * 128, 128), 128)
            for t in range(tiles):
                tat = slice(t * length, (t + 1) * length)
                qp, kp, vp = q[tat, at], kv[tat, at], kv[tat, vat]
                keys = jnp.concatenate([kp * ones_a, kp * ones_b], axis=0)
                vals = jnp.concatenate([vp * ones_a, vp * ones_b], axis=0)
                vals = jnp.concatenate([vals, ones], axis=1)
                s = lax.dot_general(
                    qp, keys, (((1,), (1,)), ((), ())), preferred_element_type=jnp.float32
                )
                parts = []
                for half in range(2):
                    sh = s[:, half * length : (half + 1) * length]
                    top = jnp.max(sh, axis=1, keepdims=True)
                    parts.append(jnp.exp((sh - top) * scale).astype(jnp.bfloat16))
                w = jnp.concatenate(parts, axis=1)
                o = jnp.dot(w, vals, preferred_element_type=jnp.float32)
                ctx[tat, at] = (o[:, :128] / o[:, 128:]).astype(jnp.bfloat16)
            return 0

        lax.fori_loop(0, width // 128, attend, 0)

        ready(3)

        def project_out(n, _):
            at = pl.ds(pl.multiple_of(n * COLS, COLS), COLS)
            y = jnp.dot(ctx[...], columns(3, n), preferred_element_type=jnp.float32)
            for t in range(tiles):
                xt = x_ref[t, :, at].astype(jnp.float32)
                yt = xt + y[t * length : (t + 1) * length]
                out_ref[t, :, at] = jnp.where(step * tiles + t < live, yt, 0.0).astype(jnp.bfloat16)
            return 0

        lax.fori_loop(0, width // COLS, project_out, 0)
        for t in range(tiles):
            emb_ref[t] = norm_rows(out_ref[t, 0:16, :], gain_ref[1:2, :])[0:1]

    @pl.when(step * tiles >= live)
    def _():
        for m in range(4):
            ready(m)
        out_ref[...] = jnp.zeros_like(out_ref)
        emb_ref[...] = jnp.zeros_like(emb_ref)


def encode_tiles(live, tiles, gain, weights):
    slots, length, width = tiles.shape
    rows = GROUP * length
    whole = pl.BlockSpec(memory_space=pltpu.VMEM)
    return pl.pallas_call(
        tile_kernel,
        grid_spec=pltpu.PrefetchScalarGridSpec(
            num_scalar_prefetch=1,
            grid=(slots // GROUP,),
            in_specs=[
                pl.BlockSpec((GROUP, length, width), lambda i, live: (i, 0, 0)),
                whole,
                pl.BlockSpec(memory_space=pl.ANY),
            ],
            out_specs=[
                pl.BlockSpec((GROUP, length, width), lambda i, live: (i, 0, 0)),
                pl.BlockSpec((GROUP, 1, width), lambda i, live: (i, 0, 0)),
            ],
            scratch_shapes=[
                pltpu.VMEM((4, width // 128, width, 128), jnp.bfloat16),
                pltpu.VMEM((rows, width), jnp.bfloat16),
                pltpu.VMEM((rows, width), jnp.bfloat16),
                pltpu.VMEM((rows, 2 * width), jnp.bfloat16),
                pltpu.VMEM((rows, width), jnp.bfloat16),
                pltpu.SemaphoreType.DMA((4,)),
            ],
        ),
        out_shape=[
            jax.ShapeDtypeStruct((slots, length, width), jnp.bfloat16),
            jax.ShapeDtypeStruct((slots, 1, width), jnp.float32),
        ],
        compiler_params=pltpu.CompilerParams(vmem_limit_bytes=56 * 1024 * 1024),
        name="tile_layer",
    )(live, tiles, gain, weights)


def partial_softmax(query_rows, key_rows, value_rows, score_scale):
    rows = query_rows.shape[0]
    block = min(512, rows)
    grouped = query_rows.reshape(rows // block, block, query_rows.shape[1], query_rows.shape[2])

    def one_block(block_rows):
        scores = (
            jnp.einsum("qhe,khe->hqk", block_rows, key_rows, preferred_element_type=jnp.float32)
            * score_scale
        )
        highest = jnp.max(scores, axis=2)
        weights = jnp.exp(scores - highest[:, :, None])
        totals = jnp.sum(weights, axis=2)
        numer = jnp.einsum(
            "hqk,khe->hqe",
            weights.astype(jnp.bfloat16),
            value_rows,
            preferred_element_type=jnp.float32,
        )
        return (highest, totals, numer)

    highest, totals, numer = lax.map(one_block, grouped)
    heads_here = query_rows.shape[1]
    highest = jnp.transpose(highest, (1, 0, 2)).reshape(heads_here, rows)
    totals = jnp.transpose(totals, (1, 0, 2)).reshape(heads_here, rows)
    numer = jnp.transpose(numer, (1, 0, 2, 3)).reshape(heads_here, rows, query_rows.shape[2])
    return (highest, totals, numer)


def combine_levels(near, far, offsets):
    near_top, near_total, near_numer = near
    far_top, far_total, far_numer = far
    rows = near_top.shape[1]
    phase = jnp.arange(rows, dtype=jnp.int32) % RATE
    picked = phase[None, :] == offsets[:, None]
    far_top_rows = jnp.repeat(far_top, RATE, axis=1)
    far_total_rows = jnp.repeat(far_total, RATE, axis=1)
    far_numer_rows = jnp.repeat(far_numer, RATE, axis=1)
    highest = jnp.where(picked, jnp.maximum(near_top, far_top_rows), near_top)
    near_factor = jnp.exp(near_top - highest)
    far_factor = jnp.where(picked, jnp.exp(jnp.minimum(far_top_rows - highest, 0.0)), 0.0)
    numer = near_numer * near_factor[:, :, None] + far_numer_rows * far_factor[:, :, None]
    totals = near_total * near_factor + far_total_rows * far_factor
    return numer / totals[:, :, None]


def per_device(
    tile_tokens,
    tile_gain,
    tile_wq,
    tile_wkv,
    tile_wo,
    slide_proj,
    slide_cache,
    slide_gain,
    slide_qkv,
    send_map,
):
    local_tiles = tile_tokens[0, 0]
    slot_count = local_tiles.shape[0]
    seq_index = lax.axis_index("seq")
    head_index = lax.axis_index("head")
    weights = gather_weights(tile_wq, tile_wkv, tile_wo)
    width = local_tiles.shape[2]
    weights = weights.reshape(4, width // 128, width, 128)
    row_plan = lax.dynamic_index_in_dim(send_map, seq_index, 1, keepdims=False)
    live_count = jnp.sum(row_plan, axis=1)
    own_live = lax.dynamic_slice_in_dim(live_count, head_index, 1, 0)
    tile_layers, embedded = encode_tiles(own_live, local_tiles, tile_gain, weights)
    slot_rows = embedded[:, 0].astype(jnp.bfloat16)
    fresh = jnp.dot(slot_rows, slide_proj, preferred_element_type=jnp.float32).astype(jnp.bfloat16)
    shared = lax.all_gather(fresh[None], "head", axis=0, tiled=True)
    groups = shared.shape[0]
    slide_width = shared.shape[2]
    span = groups * slot_count
    places = jnp.arange(slot_count, dtype=jnp.int32)
    live = (places[None, :] < live_count[:, None]).reshape(span)
    head_part = jnp.where(live[:, None], shared.reshape(span, slide_width), slide_cache[:span])
    slide_input = jnp.concatenate([head_part, slide_cache[span:]], axis=0)
    seq_rows = slide_input.shape[0]
    normed = norm_rows(slide_input, slide_gain).astype(jnp.bfloat16)
    projected = jnp.einsum(
        "tf,cfe->cte", normed, slide_qkv, preferred_element_type=jnp.float32
    ).astype(jnp.bfloat16)
    heads_here = slide_qkv.shape[2] // SLIDE_HEAD_SIZE
    query_rows = projected[0].reshape(seq_rows, heads_here, SLIDE_HEAD_SIZE)
    key_rows = projected[1].reshape(seq_rows, heads_here, SLIDE_HEAD_SIZE)
    value_rows = projected[2].reshape(seq_rows, heads_here, SLIDE_HEAD_SIZE)
    score_scale = 1.0 / math.sqrt(SLIDE_HEAD_SIZE)
    near = partial_softmax(query_rows, key_rows, value_rows, score_scale)
    offsets = (head_index * heads_here + jnp.arange(heads_here, dtype=jnp.int32)) % RATE
    selector = (offsets[:, None] == jnp.arange(RATE, dtype=jnp.int32)[None, :]).astype(jnp.bfloat16)

    def thin_rows(values):
        grouped = values.reshape(seq_rows // RATE, RATE, heads_here, SLIDE_HEAD_SIZE)
        return jnp.einsum(
            "rphe,hp->rhe", grouped, selector, preferred_element_type=jnp.float32
        ).astype(jnp.bfloat16)

    sparse_query = thin_rows(query_rows)
    both = jnp.concatenate([thin_rows(key_rows), thin_rows(value_rows)], axis=2)
    both = lax.all_gather(both, "seq", axis=0, tiled=True)
    far = partial_softmax(
        sparse_query, both[:, :, :SLIDE_HEAD_SIZE], both[:, :, SLIDE_HEAD_SIZE:], score_scale
    )
    merged = combine_levels(near, far, offsets)
    context = (
        jnp.transpose(merged, (1, 0, 2))
        .reshape(seq_rows, heads_here * SLIDE_HEAD_SIZE)
        .astype(jnp.bfloat16)
    )
    return (context, tile_layers[None, None])


def solution(mesh):
    return jax.shard_map(
        per_device,
        mesh=mesh,
        in_specs=(
            P("seq", "head", None, None, None),
            P(),
            P(("seq", "head"), None),
            P(("seq", "head"), None),
            P(("seq", "head"), None),
            P(),
            P("seq", None),
            P(),
            P(None, None, "head"),
            P(),
        ),
        out_specs=(P("seq", "head"), P("seq", "head", None, None, None)),
        check_vma=False,
    )
```

```python
import math

import jax
import jax.numpy as jnp
from jax import lax
from jax.experimental import pallas as pl
from jax.experimental.pallas import tpu as pltpu
from jax.sharding import PartitionSpec as P

TILE_HEAD_SIZE = 64
SLIDE_HEAD_SIZE = 48
RATE = 16
EPS = 1e-05
GROUP = 4
COLS = 512
MESH = pl.DeviceIdType.MESH
ORDERS = (("x", "y", "z"), ("y", "z", "x"), ("z", "x", "y"))
RING = 4


class Place:
    def __init__(self):
        seq, head = lax.axis_index("seq"), lax.axis_index("head")
        self.core = head % 2
        self.at = {"x": head // 2, "y": seq // RING, "z": seq % RING}

    def device(self, axis=None, shift=0, core=None):
        at = dict(self.at)
        if axis is not None:
            at[axis] = (at[axis] + shift) % RING
        core = self.core if core is None else core
        return (at["y"] * RING + at["z"], at["x"] * 2 + core)

    def index(self, matrix, core, part, phase, shift):
        order = ORDERS[part]
        at = {}
        for number, axis in enumerate(order):
            if number < phase:
                at[axis] = None
            elif number == phase:
                at[axis] = (self.at[axis] + shift) % RING
            else:
                at[axis] = self.at[axis]
        every = slice(None)
        x, y, z = at["x"], at["y"], at["z"]
        low, high = (every, every) if x is None else (x % 2, x // 2)
        return (
            matrix,
            low,
            core,
            part,
            every if y is None else y,
            every if z is None else z,
            high,
        )


def gather_kernel(w_ref, full, inbox, own, swap_send, swap_recv, send, recv, pair_send, pair_recv, keep):
    here = Place()
    core, other = here.core, 1 - here.core
    x = here.at["x"]
    low = x % 2
    mate = x + 1 - 2 * low
    spot = here.device()[0]
    members = [(spot, x * 2 + other), (spot, mate * 2 + core), (spot, mate * 2 + other)]
    me = 2 * low + core
    ids = [2 * low + other, 2 * (1 - low) + core, 2 * (1 - low) + other]

    barrier = pltpu.get_barrier_semaphore()
    partners = [here.device(a, s) for a in "xyz" for s in (1, 3)] + [members[0], members[2]]
    for partner in partners:
        pl.semaphore_signal(barrier, inc=1, device_id=partner, device_id_type=MESH)
    pl.semaphore_wait(barrier, len(partners))

    swaps = []
    for n in range(3):
        swaps.append(
            pltpu.make_async_remote_copy(
                src_ref=w_ref.at[ids[n]],
                dst_ref=inbox.at[n],
                send_sem=swap_send.at[n],
                recv_sem=swap_recv.at[n],
                device_id=members[n],
                device_id_type=MESH,
            )
        )
        swaps[n].start()
    for n in range(3):
        swaps[n].wait_recv()
    count = 4 * 48
    row = lax.broadcasted_iota(jnp.int32, (count, count), 0)
    col = lax.broadcasted_iota(jnp.int32, (count, count), 1)
    matrix, member, inner = row // 48, (row % 48) // 12, row % 12
    total = None
    sources = [w_ref[me]] + [inbox[n] for n in range(3)]
    names = [me] + ids
    for piece, name in zip(sources, names):
        want = matrix * 12 + inner
        pick = jnp.where((member == name) & (want == col), 1.0, 0.0).astype(jnp.bfloat16)[:, :48]
        term = jnp.dot(pick, piece, preferred_element_type=jnp.float32)
        total = term if total is None else total + term
    for m in range(4):
        for p in range(3):
            own[m, p] = total[m * 48 : (m + 1) * 48, p * 128 : (p + 1) * 128].astype(jnp.bfloat16)

    def move(m, p, phase, piece, origin, target):
        spots = here.index(m, core, p, phase, origin)
        axis = ORDERS[p][phase]
        src = own.at[m, p] if phase == 0 and origin == 0 else full.at[spots]
        return pltpu.make_async_remote_copy(
            src_ref=src,
            dst_ref=full.at[spots],
            send_sem=send.at[m, p, phase, piece],
            recv_sem=recv.at[m, p, phase, piece],
            device_id=here.device(axis, target),
            device_id_type=MESH,
        )

    def arrive(m, p, phase, piece, origin):
        spots = here.index(m, core, p, phase, origin)
        axis = ORDERS[p][phase]
        pltpu.make_async_remote_copy(
            src_ref=full.at[spots],
            dst_ref=full.at[spots],
            send_sem=send.at[m, p, phase, piece],
            recv_sem=recv.at[m, p, phase, piece],
            device_id=here.device(axis, 1),
            device_id_type=MESH,
        ).wait_recv()

    def pair(m, p, piece, phase, origin, side):
        spots = here.index(m, side, p, phase, origin)
        return pltpu.make_async_remote_copy(
            src_ref=full.at[spots],
            dst_ref=full.at[spots],
            send_sem=pair_send.at[m, p, piece],
            recv_sem=pair_recv.at[m, p, piece],
            device_id=members[0],
            device_id_type=MESH,
        )

    sent = []

    def go(copy):
        copy.start()
        sent.append(copy)

    todo = [(m, p) for m in range(4) for p in range(3)]
    keeps = []
    for m, p in todo:
        go(move(m, p, 0, 0, 0, 1))
        go(move(m, p, 0, 1, 0, 3))
    for m, p in todo:
        copy = pltpu.make_async_copy(own.at[m, p], full.at[here.index(m, core, p, 0, 0)], keep.at[m, p])
        copy.start()
        keeps.append(copy)
    for copy in keeps:
        copy.wait()
    for phase in range(3):
        for m, p in todo:
            arrive(m, p, phase, 0, 3)
            arrive(m, p, phase, 1, 1)
            if m % 2 == 0:
                go(move(m, p, phase, 2, 3, 1))
            else:
                go(move(m, p, phase, 2, 1, 3))
            if phase == 2:
                go(pair(m, p, 1, 2, 3, core))
                go(pair(m, p, 2, 2, 1, core))
        for m, p in todo:
            arrive(m, p, phase, 2, 2)
            if phase < 2:
                go(move(m, p, phase + 1, 0, 0, 1))
                go(move(m, p, phase + 1, 1, 0, 3))
            if phase == 1:
                go(pair(m, p, 0, 2, 0, core))
            if phase == 2:
                go(pair(m, p, 3, 2, 2, core))
    for m, p in todo:
        for piece, origin in enumerate((0, 3, 1, 2)):
            pair(m, p, piece, 2, origin, other).wait_recv()
    for copy in swaps + sent:
        copy.wait_send()


def gather_weights(wq, wkv, wo):
    rows, width = wq.shape
    parts = jnp.concatenate([wkv, wq, wo], axis=1)
    parts = parts.reshape(rows, 4, 4, width // 4)
    parts = jnp.transpose(parts, (2, 1, 0, 3)).reshape(4, 4 * rows, width // 4)
    dma = pltpu.SemaphoreType.DMA
    return pl.pallas_call(
        gather_kernel,
        in_specs=[pl.BlockSpec(memory_space=pltpu.VMEM)],
        out_specs=pl.BlockSpec(memory_space=pl.ANY),
        out_shape=jax.ShapeDtypeStruct((4, 2, 2, 3, 4, 4, 2, 48, 128), jnp.bfloat16),
        scratch_shapes=[
            pltpu.VMEM((3, 48, 384), jnp.bfloat16),
            pltpu.VMEM((4, 3, 48, 128), jnp.bfloat16),
            dma((3,)),
            dma((3,)),
            dma((4, 3, 3, 3)),
            dma((4, 3, 3, 3)),
            dma((4, 3, 4)),
            dma((4, 3, 4)),
            dma((4, 3)),
        ],
        compiler_params=pltpu.CompilerParams(collective_id=0, has_side_effects=True, vmem_limit_bytes=40 * 1024 * 1024),
        name="weight_gather",
    )(parts)


def norm_rows(values, gain):
    values = values.astype(jnp.float32)
    center = values - jnp.mean(values, axis=-1, keepdims=True)
    spread = jnp.mean(center * center, axis=-1, keepdims=True)
    return center * lax.rsqrt(spread + EPS) * gain


def tile_kernel(live_ref, x_ref, gain_ref, w_ref, out_ref, emb_ref, w, xn, q, kv, ctx, load):
    step = pl.program_id(0)
    live = live_ref[0]
    tiles, length, width = x_ref.shape
    blocks = COLS // 128
    loads = [pltpu.make_async_copy(w_ref.at[m], w.at[m], load.at[m]) for m in range(4)]

    @pl.when(step == 0)
    def _():
        for copy in loads:
            copy.start()

    def ready(m):
        @pl.when(step == 0)
        def _():
            loads[m].wait()

    def columns(m, n):
        return jnp.concatenate([w[m, n * blocks + j] for j in range(blocks)], axis=1)

    @pl.when(step * tiles < live)
    def _():
        for t in range(tiles):

            def norm(r, _):
                at = pl.ds(pl.multiple_of(r * 32, 32), 32)
                values = norm_rows(x_ref[t, at, :], gain_ref[0:1, :])
                xn[pl.ds(pl.multiple_of(t * length + r * 32, 32), 32), :] = values.astype(jnp.bfloat16)
                return 0

            lax.fori_loop(0, length // 32, norm, 0)

        for m, ref, base in ((0, kv, 0), (1, kv, width), (2, q, 0)):
            ready(m)

            def project(n, _):
                at = pl.ds(pl.multiple_of(base + n * COLS, COLS), COLS)
                ref[:, at] = jnp.dot(
                    xn[...], columns(m, n), preferred_element_type=jnp.float32
                ).astype(jnp.bfloat16)
                return 0

            lax.fori_loop(0, width // COLS, project, 0)

        lane = lax.broadcasted_iota(jnp.int32, (length, 128), 1)
        first = lane < TILE_HEAD_SIZE
        ones_a = jnp.where(first, 1.0, 0.0).astype(jnp.bfloat16)
        ones_b = jnp.where(first, 0.0, 1.0).astype(jnp.bfloat16)
        ones = jnp.concatenate([ones_a, ones_b], axis=0)
        scale = 1.0 / math.sqrt(TILE_HEAD_SIZE)

        def attend(p, _):
            at = pl.ds(pl.multiple_of(p * 128, 128), 128)
            vat = pl.ds(pl.multiple_of(width + p * 128, 128), 128)
            for t in range(tiles):
                tat = slice(t * length, (t + 1) * length)
                qp, kp, vp = q[tat, at], kv[tat, at], kv[tat, vat]
                keys = jnp.concatenate([kp * ones_a, kp * ones_b], axis=0)
                vals = jnp.concatenate([vp * ones_a, vp * ones_b], axis=0)
                vals = jnp.concatenate([vals, ones], axis=1)
                s = lax.dot_general(
                    qp, keys, (((1,), (1,)), ((), ())), preferred_element_type=jnp.float32
                )
                parts = []
                for half in range(2):
                    sh = s[:, half * length : (half + 1) * length]
                    top = jnp.max(sh, axis=1, keepdims=True)
                    parts.append(jnp.exp((sh - top) * scale).astype(jnp.bfloat16))
                w = jnp.concatenate(parts, axis=1)
                o = jnp.dot(w, vals, preferred_element_type=jnp.float32)
                ctx[tat, at] = (o[:, :128] / o[:, 128:]).astype(jnp.bfloat16)
            return 0

        lax.fori_loop(0, width // 128, attend, 0)

        ready(3)

        def project_out(n, _):
            at = pl.ds(pl.multiple_of(n * COLS, COLS), COLS)
            y = jnp.dot(ctx[...], columns(3, n), preferred_element_type=jnp.float32)
            for t in range(tiles):
                xt = x_ref[t, :, at].astype(jnp.float32)
                yt = xt + y[t * length : (t + 1) * length]
                out_ref[t, :, at] = jnp.where(step * tiles + t < live, yt, 0.0).astype(jnp.bfloat16)
            return 0

        lax.fori_loop(0, width // COLS, project_out, 0)
        for t in range(tiles):
            emb_ref[t] = norm_rows(out_ref[t, 0:16, :], gain_ref[1:2, :])[0:1]

    @pl.when(step * tiles >= live)
    def _():
        for m in range(4):
            ready(m)
        out_ref[...] = jnp.zeros_like(out_ref)
        emb_ref[...] = jnp.zeros_like(emb_ref)


def encode_tiles(live, tiles, gain, weights):
    slots, length, width = tiles.shape
    rows = GROUP * length
    whole = pl.BlockSpec(memory_space=pltpu.VMEM)
    return pl.pallas_call(
        tile_kernel,
        grid_spec=pltpu.PrefetchScalarGridSpec(
            num_scalar_prefetch=1,
            grid=(slots // GROUP,),
            in_specs=[
                pl.BlockSpec((GROUP, length, width), lambda i, live: (i, 0, 0)),
                whole,
                pl.BlockSpec(memory_space=pl.ANY),
            ],
            out_specs=[
                pl.BlockSpec((GROUP, length, width), lambda i, live: (i, 0, 0)),
                pl.BlockSpec((GROUP, 1, width), lambda i, live: (i, 0, 0)),
            ],
            scratch_shapes=[
                pltpu.VMEM((4, width // 128, width, 128), jnp.bfloat16),
                pltpu.VMEM((rows, width), jnp.bfloat16),
                pltpu.VMEM((rows, width), jnp.bfloat16),
                pltpu.VMEM((rows, 2 * width), jnp.bfloat16),
                pltpu.VMEM((rows, width), jnp.bfloat16),
                pltpu.SemaphoreType.DMA((4,)),
            ],
        ),
        out_shape=[
            jax.ShapeDtypeStruct((slots, length, width), jnp.bfloat16),
            jax.ShapeDtypeStruct((slots, 1, width), jnp.float32),
        ],
        compiler_params=pltpu.CompilerParams(vmem_limit_bytes=56 * 1024 * 1024),
        name="tile_layer",
    )(live, tiles, gain, weights)


def slide_kernel(
    emb_ref, proj_ref, cache_ref, gain_ref, w_ref, live_ref, out_ref,
    fresh, far, qkv, near, fresh_send, fresh_recv, far_send, far_recv,
):
    seq, head = lax.axis_index("seq"), lax.axis_index("head")
    groups, slots, width = fresh.shape
    seqs = far.shape[0]
    rows = cache_ref.shape[0]
    span = groups * slots
    heads = [(seq, (head + j) % groups) for j in range(1, groups)]
    spots = [((seq + j) % seqs, head) for j in range(1, seqs)]
    barrier = pltpu.get_barrier_semaphore()
    for partner in heads + spots:
        pl.semaphore_signal(barrier, inc=1, device_id=partner, device_id_type=MESH)

    value = jnp.dot(
        emb_ref[...].astype(jnp.bfloat16), proj_ref[...], preferred_element_type=jnp.float32
    )
    fresh[pl.ds(head, 1)] = value.astype(jnp.bfloat16)[None]
    pl.semaphore_wait(barrier, len(heads) + len(spots))

    def fresh_copy(j, slot):
        return pltpu.make_async_remote_copy(
            src_ref=fresh.at[slot],
            dst_ref=fresh.at[slot],
            send_sem=fresh_send.at[j],
            recv_sem=fresh_recv.at[j],
            device_id=heads[j],
            device_id_type=MESH,
        )

    def far_copy(j, slot):
        return pltpu.make_async_remote_copy(
            src_ref=far.at[slot],
            dst_ref=far.at[slot],
            send_sem=far_send.at[j],
            recv_sem=far_recv.at[j],
            device_id=spots[j],
            device_id_type=MESH,
        )

    for j in range(groups - 1):
        fresh_copy(j, head).start()

    def project(values):
        normed = norm_rows(values, gain_ref[...]).astype(jnp.bfloat16)
        return jnp.dot(normed, w_ref[...], preferred_element_type=jnp.float32).astype(jnp.bfloat16)

    def cached(n, _):
        at = pl.ds(pl.multiple_of(n * 128, 128), 128)
        qkv[at, :] = project(cache_ref[at, :])
        return 0

    lax.fori_loop(span // 128, rows // 128, cached, 0)
    for j in range(groups - 1):
        fresh_copy(j, (head + groups - 1 - j) % groups).wait_recv()
    mixed = jnp.where(
        live_ref[...] > 0,
        fresh[...].reshape(span, width).astype(jnp.float32),
        cache_ref[0:span, :].astype(jnp.float32),
    )
    qkv[0:span, :] = project(mixed)

    lane = lax.broadcasted_iota(jnp.int32, (1, 128), 1)
    first = lane < SLIDE_HEAD_SIZE
    thin = rows // RATE
    pick_row = lax.broadcasted_iota(jnp.int32, (2 * thin, rows), 0)
    pick_col = lax.broadcasted_iota(jnp.int32, (2 * thin, rows), 1)
    offset = (2 * head + pick_row // thin) % RATE
    pick = jnp.where(pick_col == (pick_row % thin) * RATE + offset, 1.0, 0.0).astype(jnp.bfloat16)
    sparse = jnp.dot(pick, qkv[...], preferred_element_type=jnp.float32)
    split = lax.broadcasted_iota(jnp.int32, (2 * thin, 128), 0) < thin
    lanes2 = lax.broadcasted_iota(jnp.int32, (2 * thin, 128), 1)
    own_lane = (lanes2 < SLIDE_HEAD_SIZE) == split
    sparse_query = jnp.where(own_lane, sparse[:, :128], 0.0).astype(jnp.bfloat16)
    pairs = []
    for c in (1, 2):
        values = sparse[:, c * 128 : (c + 1) * 128]
        pairs.append(jnp.where(first, values[:thin], values[thin:]))
    far[pl.ds(seq, 1)] = jnp.concatenate(pairs, axis=1).astype(jnp.bfloat16)[None]
    for j in range(seqs - 1):
        far_copy(j, seq).start()

    scale = 1.0 / math.sqrt(SLIDE_HEAD_SIZE)
    ones = jnp.ones((rows, 128), jnp.bfloat16)

    def soften(scores):
        top = jnp.max(scores, axis=1, keepdims=True)
        return jnp.exp((scores - top) * scale).astype(jnp.bfloat16)

    def near_block(n, _):
        at = pl.ds(pl.multiple_of(n * 256, 256), 256)
        parts = []
        values = jnp.concatenate([qkv[:, 256:384], ones], axis=1)
        for side in (first, jnp.logical_not(first)):
            query = qkv[at, 0:128] * jnp.where(side, 1.0, 0.0).astype(jnp.bfloat16)
            scores = lax.dot_general(
                query, qkv[:, 128:256], (((1,), (1,)), ((), ())), preferred_element_type=jnp.float32
            )
            o = jnp.dot(soften(scores), values, preferred_element_type=jnp.float32)
            parts.append(o[:, :128] / o[:, 128:])
        near[at, :] = jnp.where(first, parts[0], parts[1])
        return 0

    lax.fori_loop(0, rows // 256, near_block, 0)

    for j in range(seqs - 1):
        far_copy(j, (seq + seqs - 1 - j) % seqs).wait_recv()
    everyone = far[...].reshape(seqs * thin, 256)
    keys = jnp.concatenate([qkv[:, 128:256], everyone[:, :128]], axis=0)
    values = jnp.concatenate([qkv[:, 256:384], everyone[:, 128:]], axis=0)
    values = jnp.concatenate([values, jnp.ones((rows + seqs * thin, 128), jnp.bfloat16)], axis=1)
    scores = lax.dot_general(
        sparse_query, keys, (((1,), (1,)), ((), ())), preferred_element_type=jnp.float32
    )
    o = jnp.dot(soften(scores), values, preferred_element_type=jnp.float32)
    both = jnp.where(own_lane, o[:, :128] / o[:, 128:], 0.0).astype(jnp.bfloat16)
    place_row = lax.broadcasted_iota(jnp.int32, (rows, 2 * thin), 0)
    place_col = lax.broadcasted_iota(jnp.int32, (rows, 2 * thin), 1)
    offset = (2 * head + place_col // thin) % RATE
    place = jnp.where(place_row == (place_col % thin) * RATE + offset, 1.0, 0.0).astype(jnp.bfloat16)
    spread = jnp.dot(place, both, preferred_element_type=jnp.float32)
    row = lax.broadcasted_iota(jnp.int32, (rows, 128), 0)
    side = lax.broadcasted_iota(jnp.int32, (rows, 128), 1) // SLIDE_HEAD_SIZE
    picked = row % RATE == (2 * head + side) % RATE
    result = jnp.where(picked, spread, near[...]).astype(jnp.bfloat16)
    out_ref[...] = result[:, : out_ref.shape[1]]
    for j in range(groups - 1):
        fresh_copy(j, head).wait_send()
    for j in range(seqs - 1):
        far_copy(j, seq).wait_send()


def encode_slide(embedded, proj, cache, gain, weights, live, groups, seqs):
    slots, width = embedded.shape[0], proj.shape[1]
    rows, columns = cache.shape[0], weights.shape[2]
    padded = jnp.pad(weights, ((0, 0), (0, 0), (0, 128 - columns)))
    padded = jnp.transpose(padded, (1, 0, 2)).reshape(width, 3 * 128)
    dma = pltpu.SemaphoreType.DMA
    vmem = pl.BlockSpec(memory_space=pltpu.VMEM)
    return pl.pallas_call(
        slide_kernel,
        in_specs=[vmem] * 6,
        out_specs=vmem,
        out_shape=jax.ShapeDtypeStruct((rows, columns), jnp.bfloat16),
        scratch_shapes=[
            pltpu.VMEM((groups, slots, width), jnp.bfloat16),
            pltpu.VMEM((seqs, rows // RATE, 256), jnp.bfloat16),
            pltpu.VMEM((rows, 3 * 128), jnp.bfloat16),
            pltpu.VMEM((rows, 128), jnp.float32),
            dma((groups - 1,)),
            dma((groups - 1,)),
            dma((seqs - 1,)),
            dma((seqs - 1,)),
        ],
        compiler_params=pltpu.CompilerParams(
            collective_id=1, has_side_effects=True, vmem_limit_bytes=48 * 1024 * 1024
        ),
        name="slide_layer",
    )(embedded, proj, cache, gain, padded, live)


def per_device(
    tile_tokens,
    tile_gain,
    tile_wq,
    tile_wkv,
    tile_wo,
    slide_proj,
    slide_cache,
    slide_gain,
    slide_qkv,
    send_map,
):
    local_tiles = tile_tokens[0, 0]
    slot_count = local_tiles.shape[0]
    seq_index = lax.axis_index("seq")
    head_index = lax.axis_index("head")
    weights = gather_weights(tile_wq, tile_wkv, tile_wo)
    width = local_tiles.shape[2]
    weights = weights.reshape(4, width // 128, width, 128)
    row_plan = lax.dynamic_index_in_dim(send_map, seq_index, 1, keepdims=False)
    live_count = jnp.sum(row_plan, axis=1)
    own_live = lax.dynamic_slice_in_dim(live_count, head_index, 1, 0)
    tile_layers, embedded = encode_tiles(own_live, local_tiles, tile_gain, weights)
    groups, seqs = send_map.shape[0], send_map.shape[1]
    places = jnp.arange(slot_count, dtype=jnp.int32)
    live = (places[None, :] < live_count[:, None]).reshape(groups * slot_count, 1).astype(jnp.float32)
    context = encode_slide(
        embedded[:, 0], slide_proj, slide_cache, slide_gain[None], slide_qkv, live, groups, seqs
    )
    return (context, tile_layers[None, None])


def solution(mesh):
    return jax.shard_map(
        per_device,
        mesh=mesh,
        in_specs=(
            P("seq", "head", None, None, None),
            P(),
            P(("seq", "head"), None),
            P(("seq", "head"), None),
            P(("seq", "head"), None),
            P(),
            P("seq", None),
            P(),
            P(None, None, "head"),
            P(),
        ),
        out_specs=(P("seq", "head"), P("seq", "head", None, None, None)),
        check_vma=False,
    )
```

```python
import math

import jax
import jax.numpy as jnp
from jax import lax
from jax.experimental import pallas as pl
from jax.experimental.pallas import tpu as pltpu
from jax.sharding import PartitionSpec as P

TILE_HEAD_SIZE = 64
SLIDE_HEAD_SIZE = 48
RATE = 16
EPS = 1e-05
GROUP = 2
COLS = 512
MESH = pl.DeviceIdType.MESH
ORDERS = (("x", "y", "z"), ("y", "z", "x"), ("z", "x", "y"))
RING = 4
ROWS = 512


def norm_rows(values, gain):
    values = values.astype(jnp.float32)
    center = values - jnp.mean(values, axis=-1, keepdims=True)
    spread = jnp.mean(center * center, axis=-1, keepdims=True)
    return center * lax.rsqrt(spread + EPS) * gain


class Place:
    def __init__(self):
        seq, head = lax.axis_index("seq"), lax.axis_index("head")
        self.core = head % 2
        self.at = {"x": head // 2, "y": seq // RING, "z": seq % RING}

    def device(self, axis=None, shift=0, core=None):
        at = dict(self.at)
        if axis is not None:
            at[axis] = (at[axis] + shift) % RING
        core = self.core if core is None else core
        return (at["y"] * RING + at["z"], at["x"] * 2 + core)

    def index(self, matrix, core, part, phase, shift):
        order = ORDERS[part]
        at = {}
        for number, axis in enumerate(order):
            if number < phase:
                at[axis] = None
            elif number == phase:
                at[axis] = (self.at[axis] + shift) % RING
            else:
                at[axis] = self.at[axis]
        every = slice(None)
        x, y, z = at["x"], at["y"], at["z"]
        low, high = (every, every) if x is None else (x % 2, x // 2)
        return (
            matrix,
            low,
            core,
            part,
            every if y is None else y,
            every if z is None else z,
            high,
        )


def gather_kernel(
    w_ref, x_ref, gain_ref, kvq_ref, last_ref, full, rows_ref, stage, inbox, own,
    swap_send, swap_recv, send, recv, pair_send, pair_recv, keep, store, load,
):
    here = Place()
    length = rows_ref.shape[0]
    load_copy = pltpu.make_async_copy(x_ref, rows_ref, load)
    load_copy.start()

    def normalise(start, count):
        def step(r, _):
            at = pl.ds(pl.multiple_of(r * 32, 32), 32)
            rows_ref[at, :] = norm_rows(rows_ref[at, :], gain_ref[0:1, :]).astype(jnp.bfloat16)
            return 0

        lax.fori_loop(start, start + count, step, 0)

    def ref_of(spots):
        m = spots[0]
        return full.at[spots] if m < 3 else last_ref.at[spots[1:]]

    def store_copy(m, slot, low, block):
        return pltpu.make_async_copy(
            stage.at[slot],
            kvq_ref.at[m, pl.ds(low * 6, 6), pl.ds(pl.multiple_of(block * ROWS, ROWS), ROWS), :],
            store.at[slot],
        )

    blocks = length // ROWS

    def multiply(m, start, count):
        def step(u, _):
            slot, low, block = u % 2, u // blocks, u % blocks

            @pl.when(m * 2 * blocks + u >= 2)
            def _():
                store_copy(m, slot, low, block).wait()

            at = pl.ds(pl.multiple_of(block * ROWS, ROWS), ROWS)
            width = rows_ref.shape[1]
            w = jnp.concatenate(
                [full[m, low, j // 3, j % 3].reshape(width, 128) for j in range(6)], axis=1
            )
            y = jnp.dot(rows_ref[at, :], w, preferred_element_type=jnp.float32).astype(jnp.bfloat16)
            for j in range(6):
                stage[slot, j] = y[:, j * 128 : (j + 1) * 128]
            store_copy(m, slot, low, block).start()
            return 0

        lax.fori_loop(start, start + count, step, 0)
    core, other = here.core, 1 - here.core
    x = here.at["x"]
    low = x % 2
    mate = x + 1 - 2 * low
    spot = here.device()[0]
    members = [(spot, x * 2 + other), (spot, mate * 2 + core), (spot, mate * 2 + other)]
    me = 2 * low + core
    ids = [2 * low + other, 2 * (1 - low) + core, 2 * (1 - low) + other]

    barrier = pltpu.get_barrier_semaphore()
    partners = [here.device(a, s) for a in "xyz" for s in (1, 3)] + [members[0], members[2]]
    for partner in partners:
        pl.semaphore_signal(barrier, inc=1, device_id=partner, device_id_type=MESH)
    pl.semaphore_wait(barrier, len(partners))

    swaps = []
    for n in range(3):
        swaps.append(
            pltpu.make_async_remote_copy(
                src_ref=w_ref.at[ids[n]],
                dst_ref=inbox.at[n],
                send_sem=swap_send.at[n],
                recv_sem=swap_recv.at[n],
                device_id=members[n],
                device_id_type=MESH,
            )
        )
        swaps[n].start()
    load_copy.wait()
    share = -(-length // 32 // 6)
    normalise(0, share)
    for n in range(3):
        swaps[n].wait_recv()
    count = 4 * 48
    row = lax.broadcasted_iota(jnp.int32, (count, count), 0)
    col = lax.broadcasted_iota(jnp.int32, (count, count), 1)
    matrix, member, inner = row // 48, (row % 48) // 12, row % 12
    total = None
    sources = [w_ref[me]] + [inbox[n] for n in range(3)]
    names = [me] + ids
    for piece, name in zip(sources, names):
        want = matrix * 12 + inner
        pick = jnp.where((member == name) & (want == col), 1.0, 0.0).astype(jnp.bfloat16)[:, :48]
        term = jnp.dot(pick, piece, preferred_element_type=jnp.float32)
        total = term if total is None else total + term
    for m in range(4):
        for p in range(3):
            own[m, p] = total[m * 48 : (m + 1) * 48, p * 128 : (p + 1) * 128].astype(jnp.bfloat16)

    def move(m, p, phase, piece, origin, target):
        spots = here.index(m, core, p, phase, origin)
        axis = ORDERS[p][phase]
        src = own.at[m, p] if phase == 0 and origin == 0 else ref_of(spots)
        return pltpu.make_async_remote_copy(
            src_ref=src,
            dst_ref=ref_of(spots),
            send_sem=send.at[m, p, phase, piece],
            recv_sem=recv.at[m, p, phase, piece],
            device_id=here.device(axis, target),
            device_id_type=MESH,
        )

    def arrive(m, p, phase, piece, origin):
        spots = here.index(m, core, p, phase, origin)
        axis = ORDERS[p][phase]
        pltpu.make_async_remote_copy(
            src_ref=ref_of(spots),
            dst_ref=ref_of(spots),
            send_sem=send.at[m, p, phase, piece],
            recv_sem=recv.at[m, p, phase, piece],
            device_id=here.device(axis, 1),
            device_id_type=MESH,
        ).wait_recv()

    def pair(m, p, piece, phase, origin, side):
        spots = here.index(m, side, p, phase, origin)
        return pltpu.make_async_remote_copy(
            src_ref=ref_of(spots),
            dst_ref=ref_of(spots),
            send_sem=pair_send.at[m, p, piece],
            recv_sem=pair_recv.at[m, p, piece],
            device_id=members[0],
            device_id_type=MESH,
        )

    sent = []

    def go(copy):
        copy.start()
        sent.append(copy)

    todo = [(m, p) for m in range(4) for p in range(3)]
    keeps = []
    for m, p in todo:
        go(move(m, p, 0, 0, 0, 1))
        go(move(m, p, 0, 1, 0, 3))
    for m, p in todo:
        copy = pltpu.make_async_copy(own.at[m, p], ref_of(here.index(m, core, p, 0, 0)), keep.at[m, p])
        copy.start()
        keeps.append(copy)
    for copy in keeps:
        copy.wait()
    done = [share]

    def norm_some():
        count = min(share, length // 32 - done[0])
        normalise(done[0], count)
        done[0] += count

    def first_arrivals(m, p, phase):
        arrive(m, p, phase, 0, 3)
        arrive(m, p, phase, 1, 1)
        if m % 2 == 0:
            go(move(m, p, phase, 2, 3, 1))
        else:
            go(move(m, p, phase, 2, 1, 3))
        if phase == 2:
            go(pair(m, p, 1, 2, 3, core))
            go(pair(m, p, 2, 2, 1, core))

    def start_phase(m, p, phase):
        go(move(m, p, phase, 0, 0, 1))
        go(move(m, p, phase, 1, 0, 3))

    def last_arrival(m, p, phase):
        arrive(m, p, phase, 2, 2)
        if phase == 0 or (phase == 1 and m < 2):
            start_phase(m, p, phase + 1)
        if phase == 1:
            go(pair(m, p, 0, 2, 0, core))
        if phase == 2:
            go(pair(m, p, 3, 2, 2, core))

    def from_pair(m, p):
        for piece, origin in enumerate((0, 3, 1, 2)):
            pair(m, p, piece, 2, origin, other).wait_recv()

    def every(step, m, *rest):
        for p in range(3):
            step(m, p, *rest)

    norm_some()
    for phase in range(2):
        for m in range(4):
            every(first_arrivals, m, phase)
        norm_some()
        for m in range(4):
            every(last_arrival, m, phase)
        norm_some()
    every(first_arrivals, 0, 2)
    every(start_phase, 2, 2)
    every(last_arrival, 0, 2)
    every(first_arrivals, 1, 2)
    every(start_phase, 3, 2)
    every(from_pair, 0)
    multiply(0, 0, blocks)
    every(last_arrival, 1, 2)
    multiply(0, blocks, blocks)
    every(first_arrivals, 2, 2)
    every(from_pair, 1)
    multiply(1, 0, blocks)
    every(last_arrival, 2, 2)
    multiply(1, blocks, blocks)
    every(first_arrivals, 3, 2)
    every(from_pair, 2)
    multiply(2, 0, blocks)
    every(last_arrival, 3, 2)
    multiply(2, blocks, blocks)
    every(from_pair, 3)
    for slot in range(2):
        store_copy(2, slot, 1, blocks - 2 + slot).wait()
    for copy in swaps + sent:
        copy.wait_send()


def project_tiles(tiles, gain, wq, wkv, wo):
    rows, width = wq.shape
    slots, length, _ = tiles.shape
    count = slots * length
    parts = jnp.concatenate([wkv, wq, wo], axis=1)
    parts = parts.reshape(rows, 4, 4, width // 4)
    parts = jnp.transpose(parts, (2, 1, 0, 3)).reshape(4, 4 * rows, width // 4)
    dma = pltpu.SemaphoreType.DMA
    hbm = pl.BlockSpec(memory_space=pl.ANY)
    vmem = pl.BlockSpec(memory_space=pltpu.VMEM)
    one = (2, 2, 3, 4, 4, 2, 4 * rows, 128)
    return pl.pallas_call(
        gather_kernel,
        in_specs=[vmem, hbm, vmem],
        out_specs=[hbm, hbm],
        out_shape=[
            jax.ShapeDtypeStruct((3, width // 128, count, 128), jnp.bfloat16),
            jax.ShapeDtypeStruct(one, jnp.bfloat16),
        ],
        scratch_shapes=[
            pltpu.VMEM((3,) + one, jnp.bfloat16),
            pltpu.VMEM((count, width), jnp.bfloat16),
            pltpu.VMEM((2, 6, ROWS, 128), jnp.bfloat16),
            pltpu.VMEM((3, 4 * rows, width // 4), jnp.bfloat16),
            pltpu.VMEM((4, 3, 4 * rows, 128), jnp.bfloat16),
            dma((3,)),
            dma((3,)),
            dma((4, 3, 3, 3)),
            dma((4, 3, 3, 3)),
            dma((4, 3, 4)),
            dma((4, 3, 4)),
            dma((4, 3)),
            dma((2,)),
            dma,
        ],
        compiler_params=pltpu.CompilerParams(
            collective_id=0, has_side_effects=True, vmem_limit_bytes=48 * 1024 * 1024
        ),
        name="gather_project",
    )(parts, tiles.reshape(count, width), gain)


def tile_kernel(live_ref, x_ref, gain_ref, kvq, wo_ref, out_ref, emb_ref, wo, ctx, load):
    step = pl.program_id(0)
    live = live_ref[0]
    tiles, length, width = x_ref.shape
    pairs = width // 128
    load_copy = pltpu.make_async_copy(wo_ref, wo, load)

    @pl.when(step == 0)
    def _():
        load_copy.start()

    @pl.when(step * tiles < live)
    def _():
        lane = lax.broadcasted_iota(jnp.int32, (length, 128), 1)
        first = lane < TILE_HEAD_SIZE
        ones_a = jnp.where(first, 1.0, 0.0).astype(jnp.bfloat16)
        ones_b = jnp.where(first, 0.0, 1.0).astype(jnp.bfloat16)
        ones = jnp.concatenate([ones_a, ones_b], axis=0)
        scale = math.log2(math.e) / math.sqrt(TILE_HEAD_SIZE)
        for p in range(pairs):
            for t in range(tiles):
                at = slice(t * length, (t + 1) * length)
                kp, vp, qp = kvq[0, p, at, :], kvq[1, p, at, :], kvq[2, p, at, :]
                keys = jnp.concatenate([kp * ones_a, kp * ones_b], axis=0)
                vals = jnp.concatenate([vp * ones_a, vp * ones_b], axis=0)
                vals = jnp.concatenate([vals, ones], axis=1)
                s = lax.dot_general(
                    qp, keys, (((1,), (1,)), ((), ())), preferred_element_type=jnp.float32
                )
                parts = []
                for half in range(2):
                    sh = s[:, half * length : (half + 1) * length]
                    top = jnp.max(sh, axis=1, keepdims=True)
                    parts.append(jnp.exp2((sh - top) * scale).astype(jnp.bfloat16))
                o = jnp.dot(
                    jnp.concatenate(parts, axis=1), vals, preferred_element_type=jnp.float32
                )
                ctx[p, at, :] = (o[:, :128] / o[:, 128:]).astype(jnp.bfloat16)

    @pl.when(step == 0)
    def _():
        load_copy.wait()

    @pl.when(step * tiles < live)
    def _():
        def project_out(n, _):
            at = pl.ds(pl.multiple_of(n * COLS, COLS), COLS)
            blocks = COLS // 128
            context = jnp.concatenate([ctx[j] for j in range(pairs)], axis=1)
            w = jnp.concatenate([wo[n * blocks + j] for j in range(blocks)], axis=1)
            y = jnp.dot(context, w, preferred_element_type=jnp.float32)
            for t in range(tiles):
                xt = x_ref[t, :, at].astype(jnp.float32)
                yt = xt + y[t * length : (t + 1) * length]
                out_ref[t, :, at] = jnp.where(step * tiles + t < live, yt, 0.0).astype(jnp.bfloat16)
            return 0

        lax.fori_loop(0, width // COLS, project_out, 0)
        for t in range(tiles):
            emb_ref[t] = norm_rows(out_ref[t, 0:16, :], gain_ref[1:2, :])[0:1]

    @pl.when(step * tiles >= live)
    def _():
        out_ref[...] = jnp.zeros_like(out_ref)
        emb_ref[...] = jnp.zeros_like(emb_ref)


def encode_tiles(live, tiles, gain, kvq, wo):
    slots, length, width = tiles.shape
    rows = GROUP * length
    return pl.pallas_call(
        tile_kernel,
        grid_spec=pltpu.PrefetchScalarGridSpec(
            num_scalar_prefetch=1,
            grid=(slots // GROUP,),
            in_specs=[
                pl.BlockSpec((GROUP, length, width), lambda i, live: (i, 0, 0)),
                pl.BlockSpec(memory_space=pltpu.VMEM),
                pl.BlockSpec((3, width // 128, rows, 128), lambda i, live: (0, 0, i, 0)),
                pl.BlockSpec(memory_space=pl.ANY),
            ],
            out_specs=[
                pl.BlockSpec((GROUP, length, width), lambda i, live: (i, 0, 0)),
                pl.BlockSpec((GROUP, 1, width), lambda i, live: (i, 0, 0)),
            ],
            scratch_shapes=[
                pltpu.VMEM((width // 128, width, 128), jnp.bfloat16),
                pltpu.VMEM((width // 128, rows, 128), jnp.bfloat16),
                pltpu.SemaphoreType.DMA,
            ],
        ),
        out_shape=[
            jax.ShapeDtypeStruct((slots, length, width), jnp.bfloat16),
            jax.ShapeDtypeStruct((slots, 1, width), jnp.float32),
        ],
        compiler_params=pltpu.CompilerParams(vmem_limit_bytes=48 * 1024 * 1024),
        name="tile_layer",
    )(live, tiles, gain, kvq, wo)


def slide_kernel(
    emb_ref, proj_ref, cache_ref, gain_ref, w_ref, live_ref, out_ref,
    fresh, far, qkv, near, fresh_send, fresh_recv, far_send, far_recv,
):
    seq, head = lax.axis_index("seq"), lax.axis_index("head")
    groups, slots, width = fresh.shape
    seqs = far.shape[0]
    rows = cache_ref.shape[0]
    span = groups * slots
    heads = [(seq, (head + j) % groups) for j in range(1, groups)]
    spots = [((seq + j) % seqs, head) for j in range(1, seqs)]
    barrier = pltpu.get_barrier_semaphore()
    for partner in heads + spots:
        pl.semaphore_signal(barrier, inc=1, device_id=partner, device_id_type=MESH)

    value = jnp.dot(
        emb_ref[...].astype(jnp.bfloat16), proj_ref[...], preferred_element_type=jnp.float32
    )
    fresh[pl.ds(head, 1)] = value.astype(jnp.bfloat16)[None]
    pl.semaphore_wait(barrier, len(heads) + len(spots))

    def fresh_copy(j, slot):
        return pltpu.make_async_remote_copy(
            src_ref=fresh.at[slot],
            dst_ref=fresh.at[slot],
            send_sem=fresh_send.at[j],
            recv_sem=fresh_recv.at[j],
            device_id=heads[j],
            device_id_type=MESH,
        )

    def far_copy(j, slot):
        return pltpu.make_async_remote_copy(
            src_ref=far.at[slot],
            dst_ref=far.at[slot],
            send_sem=far_send.at[j],
            recv_sem=far_recv.at[j],
            device_id=spots[j],
            device_id_type=MESH,
        )

    for j in range(groups - 1):
        fresh_copy(j, head).start()

    def project(values):
        normed = norm_rows(values, gain_ref[...]).astype(jnp.bfloat16)
        return jnp.dot(normed, w_ref[...], preferred_element_type=jnp.float32).astype(jnp.bfloat16)

    def cached(n, _):
        at = pl.ds(pl.multiple_of(n * 128, 128), 128)
        qkv[at, :] = project(cache_ref[at, :])
        return 0

    lax.fori_loop(span // 128, rows // 128, cached, 0)
    for j in range(groups - 1):
        fresh_copy(j, (head + groups - 1 - j) % groups).wait_recv()
    mixed = jnp.where(
        live_ref[...] > 0,
        fresh[...].reshape(span, width).astype(jnp.float32),
        cache_ref[0:span, :].astype(jnp.float32),
    )
    qkv[0:span, :] = project(mixed)

    lane = lax.broadcasted_iota(jnp.int32, (1, 128), 1)
    first = lane < SLIDE_HEAD_SIZE
    thin = rows // RATE
    pick_row = lax.broadcasted_iota(jnp.int32, (2 * thin, rows), 0)
    pick_col = lax.broadcasted_iota(jnp.int32, (2 * thin, rows), 1)
    offset = (2 * head + pick_row // thin) % RATE
    pick = jnp.where(pick_col == (pick_row % thin) * RATE + offset, 1.0, 0.0).astype(jnp.bfloat16)
    sparse = jnp.dot(pick, qkv[...], preferred_element_type=jnp.float32)
    split = lax.broadcasted_iota(jnp.int32, (2 * thin, 128), 0) < thin
    lanes2 = lax.broadcasted_iota(jnp.int32, (2 * thin, 128), 1)
    own_lane = (lanes2 < SLIDE_HEAD_SIZE) == split
    sparse_query = jnp.where(own_lane, sparse[:, :128], 0.0).astype(jnp.bfloat16)
    pairs = []
    for c in (1, 2):
        values = sparse[:, c * 128 : (c + 1) * 128]
        pairs.append(jnp.where(first, values[:thin], values[thin:]))
    far[pl.ds(seq, 1)] = jnp.concatenate(pairs, axis=1).astype(jnp.bfloat16)[None]
    for j in range(seqs - 1):
        far_copy(j, seq).start()

    scale = 1.0 / math.sqrt(SLIDE_HEAD_SIZE)
    ones = jnp.ones((rows, 128), jnp.bfloat16)

    def soften(scores):
        top = jnp.max(scores, axis=1, keepdims=True)
        return jnp.exp((scores - top) * scale).astype(jnp.bfloat16)

    def near_block(n, _):
        at = pl.ds(pl.multiple_of(n * 256, 256), 256)
        parts = []
        values = jnp.concatenate([qkv[:, 256:384], ones], axis=1)
        for side in (first, jnp.logical_not(first)):
            query = qkv[at, 0:128] * jnp.where(side, 1.0, 0.0).astype(jnp.bfloat16)
            scores = lax.dot_general(
                query, qkv[:, 128:256], (((1,), (1,)), ((), ())), preferred_element_type=jnp.float32
            )
            o = jnp.dot(soften(scores), values, preferred_element_type=jnp.float32)
            parts.append(o[:, :128] / o[:, 128:])
        near[at, :] = jnp.where(first, parts[0], parts[1])
        return 0

    lax.fori_loop(0, rows // 256, near_block, 0)

    for j in range(seqs - 1):
        far_copy(j, (seq + seqs - 1 - j) % seqs).wait_recv()
    everyone = far[...].reshape(seqs * thin, 256)
    keys = jnp.concatenate([qkv[:, 128:256], everyone[:, :128]], axis=0)
    values = jnp.concatenate([qkv[:, 256:384], everyone[:, 128:]], axis=0)
    values = jnp.concatenate([values, jnp.ones((rows + seqs * thin, 128), jnp.bfloat16)], axis=1)
    scores = lax.dot_general(
        sparse_query, keys, (((1,), (1,)), ((), ())), preferred_element_type=jnp.float32
    )
    o = jnp.dot(soften(scores), values, preferred_element_type=jnp.float32)
    both = jnp.where(own_lane, o[:, :128] / o[:, 128:], 0.0).astype(jnp.bfloat16)
    place_row = lax.broadcasted_iota(jnp.int32, (rows, 2 * thin), 0)
    place_col = lax.broadcasted_iota(jnp.int32, (rows, 2 * thin), 1)
    offset = (2 * head + place_col // thin) % RATE
    place = jnp.where(place_row == (place_col % thin) * RATE + offset, 1.0, 0.0).astype(jnp.bfloat16)
    spread = jnp.dot(place, both, preferred_element_type=jnp.float32)
    row = lax.broadcasted_iota(jnp.int32, (rows, 128), 0)
    side = lax.broadcasted_iota(jnp.int32, (rows, 128), 1) // SLIDE_HEAD_SIZE
    picked = row % RATE == (2 * head + side) % RATE
    result = jnp.where(picked, spread, near[...]).astype(jnp.bfloat16)
    out_ref[...] = result[:, : out_ref.shape[1]]
    for j in range(groups - 1):
        fresh_copy(j, head).wait_send()
    for j in range(seqs - 1):
        far_copy(j, seq).wait_send()


def encode_slide(embedded, proj, cache, gain, weights, live, groups, seqs):
    slots, width = embedded.shape[0], proj.shape[1]
    rows, columns = cache.shape[0], weights.shape[2]
    padded = jnp.pad(weights, ((0, 0), (0, 0), (0, 128 - columns)))
    padded = jnp.transpose(padded, (1, 0, 2)).reshape(width, 3 * 128)
    dma = pltpu.SemaphoreType.DMA
    vmem = pl.BlockSpec(memory_space=pltpu.VMEM)
    return pl.pallas_call(
        slide_kernel,
        in_specs=[vmem] * 6,
        out_specs=vmem,
        out_shape=jax.ShapeDtypeStruct((rows, columns), jnp.bfloat16),
        scratch_shapes=[
            pltpu.VMEM((groups, slots, width), jnp.bfloat16),
            pltpu.VMEM((seqs, rows // RATE, 256), jnp.bfloat16),
            pltpu.VMEM((rows, 3 * 128), jnp.bfloat16),
            pltpu.VMEM((rows, 128), jnp.float32),
            dma((groups - 1,)),
            dma((groups - 1,)),
            dma((seqs - 1,)),
            dma((seqs - 1,)),
        ],
        compiler_params=pltpu.CompilerParams(
            collective_id=1, has_side_effects=True, vmem_limit_bytes=48 * 1024 * 1024
        ),
        name="slide_layer",
    )(embedded, proj, cache, gain, padded, live)


def per_device(
    tile_tokens,
    tile_gain,
    tile_wq,
    tile_wkv,
    tile_wo,
    slide_proj,
    slide_cache,
    slide_gain,
    slide_qkv,
    send_map,
):
    local_tiles = tile_tokens[0, 0]
    slot_count = local_tiles.shape[0]
    seq_index = lax.axis_index("seq")
    head_index = lax.axis_index("head")
    kvq, w_out = project_tiles(local_tiles, tile_gain, tile_wq, tile_wkv, tile_wo)
    w_out = w_out.reshape(kvq.shape[1], -1, 128)
    row_plan = lax.dynamic_index_in_dim(send_map, seq_index, 1, keepdims=False)
    live_count = jnp.sum(row_plan, axis=1)
    own_live = lax.dynamic_slice_in_dim(live_count, head_index, 1, 0)
    tile_layers, embedded = encode_tiles(own_live, local_tiles, tile_gain, kvq, w_out)
    groups, seqs = send_map.shape[0], send_map.shape[1]
    places = jnp.arange(slot_count, dtype=jnp.int32)
    live = (places[None, :] < live_count[:, None]).reshape(groups * slot_count, 1).astype(jnp.float32)
    context = encode_slide(
        embedded[:, 0], slide_proj, slide_cache, slide_gain[None], slide_qkv, live, groups, seqs
    )
    return (context, tile_layers[None, None])


def solution(mesh):
    return jax.shard_map(
        per_device,
        mesh=mesh,
        in_specs=(
            P("seq", "head", None, None, None),
            P(),
            P(("seq", "head"), None),
            P(("seq", "head"), None),
            P(("seq", "head"), None),
            P(),
            P("seq", None),
            P(),
            P(None, None, "head"),
            P(),
        ),
        out_specs=(P("seq", "head"), P("seq", "head", None, None, None)),
        check_vma=False,
    )
```

```python
import math

import jax
import jax.numpy as jnp
from jax import lax
from jax.experimental import pallas as pl
from jax.experimental.pallas import tpu as pltpu
from jax.sharding import PartitionSpec as P

TILE_HEAD_SIZE = 64
SLIDE_HEAD_SIZE = 48
RATE = 16
EPS = 1e-05
GROUP = 2
COLS = 512
MESH = pl.DeviceIdType.MESH
ORDERS = (("x", "y", "z"), ("y", "z", "x"), ("z", "x", "y"))
RING = 4
ROWS = 512


def norm_rows(values, gain):
    values = values.astype(jnp.float32)
    center = values - jnp.mean(values, axis=-1, keepdims=True)
    spread = jnp.mean(center * center, axis=-1, keepdims=True)
    return center * lax.rsqrt(spread + EPS) * gain


def project_slide(values, gain, w_ref):
    normed = norm_rows(values, gain).astype(jnp.bfloat16)
    parts = []
    for c in range(3):
        y = jnp.dot(normed, w_ref[c], preferred_element_type=jnp.float32)
        parts += [y, jnp.zeros((y.shape[0], 128 - y.shape[1]), jnp.float32)]
    return jnp.concatenate(parts, axis=1).astype(jnp.bfloat16)


class Place:
    def __init__(self):
        seq, head = lax.axis_index("seq"), lax.axis_index("head")
        self.core = head % 2
        self.at = {"x": head // 2, "y": seq // RING, "z": seq % RING}

    def device(self, axis=None, shift=0, core=None):
        at = dict(self.at)
        if axis is not None:
            at[axis] = (at[axis] + shift) % RING
        core = self.core if core is None else core
        return (at["y"] * RING + at["z"], at["x"] * 2 + core)

    def index(self, matrix, core, part, phase, shift):
        order = ORDERS[part]
        at = {}
        for number, axis in enumerate(order):
            if number < phase:
                at[axis] = None
            elif number == phase:
                at[axis] = (self.at[axis] + shift) % RING
            else:
                at[axis] = self.at[axis]
        every = slice(None)
        x, y, z = at["x"], at["y"], at["z"]
        low, high = (every, every) if x is None else (x % 2, x // 2)
        return (
            matrix,
            low,
            core,
            part,
            every if y is None else y,
            every if z is None else z,
            high,
        )


def gather_kernel(
    w_ref, x_ref, gain_ref, cache_ref, slide_gain_ref, slide_w_ref,
    kvq_ref, last_ref, slide_ref, full, rows_ref, stage, inbox, own, slide_rows,
    swap_send, swap_recv, send, recv, pair_send, pair_recv, keep, store, load, slide_store,
):
    here = Place()
    length = rows_ref.shape[0]
    load_copy = pltpu.make_async_copy(x_ref, rows_ref, load)
    load_copy.start()

    def normalise(start, count):
        def step(r, _):
            at = pl.ds(pl.multiple_of(r * 32, 32), 32)
            rows_ref[at, :] = norm_rows(rows_ref[at, :], gain_ref[0:1, :]).astype(jnp.bfloat16)
            return 0

        lax.fori_loop(start, start + count, step, 0)

    def ref_of(spots):
        m = spots[0]
        return full.at[spots] if m < 3 else last_ref.at[spots[1:]]

    def store_copy(m, slot, low, block):
        return pltpu.make_async_copy(
            stage.at[slot],
            kvq_ref.at[m, pl.ds(low * 6, 6), pl.ds(pl.multiple_of(block * ROWS, ROWS), ROWS), :],
            store.at[slot],
        )

    blocks = length // ROWS

    def multiply(m, start, count):
        def step(u, _):
            slot, low, block = u % 2, u // blocks, u % blocks

            @pl.when(m * 2 * blocks + u >= 2)
            def _():
                store_copy(m, slot, low, block).wait()

            at = pl.ds(pl.multiple_of(block * ROWS, ROWS), ROWS)
            width = rows_ref.shape[1]
            w = jnp.concatenate(
                [full[m, low, j // 3, j % 3].reshape(width, 128) for j in range(6)], axis=1
            )
            y = jnp.dot(rows_ref[at, :], w, preferred_element_type=jnp.float32).astype(jnp.bfloat16)
            for j in range(6):
                stage[slot, j] = y[:, j * 128 : (j + 1) * 128]
            store_copy(m, slot, low, block).start()
            return 0

        lax.fori_loop(start, start + count, step, 0)
    core, other = here.core, 1 - here.core
    x = here.at["x"]
    low = x % 2
    mate = x + 1 - 2 * low
    spot = here.device()[0]
    members = [(spot, x * 2 + other), (spot, mate * 2 + core), (spot, mate * 2 + other)]
    me = 2 * low + core
    ids = [2 * low + other, 2 * (1 - low) + core, 2 * (1 - low) + other]

    barrier = pltpu.get_barrier_semaphore()
    partners = [here.device(a, s) for a in "xyz" for s in (1, 3)] + [members[0], members[2]]
    for partner in partners:
        pl.semaphore_signal(barrier, inc=1, device_id=partner, device_id_type=MESH)
    pl.semaphore_wait(barrier, len(partners))

    swaps = []
    for n in range(3):
        swaps.append(
            pltpu.make_async_remote_copy(
                src_ref=w_ref.at[ids[n]],
                dst_ref=inbox.at[n],
                send_sem=swap_send.at[n],
                recv_sem=swap_recv.at[n],
                device_id=members[n],
                device_id_type=MESH,
            )
        )
        swaps[n].start()
    load_copy.wait()
    share = -(-length // 32 // 6)
    normalise(0, share)
    for n in range(3):
        swaps[n].wait_recv()
    count = 4 * 48
    row = lax.broadcasted_iota(jnp.int32, (count, count), 0)
    col = lax.broadcasted_iota(jnp.int32, (count, count), 1)
    matrix, member, inner = row // 48, (row % 48) // 12, row % 12
    total = None
    sources = [w_ref[me]] + [inbox[n] for n in range(3)]
    names = [me] + ids
    for piece, name in zip(sources, names):
        want = matrix * 12 + inner
        pick = jnp.where((member == name) & (want == col), 1.0, 0.0).astype(jnp.bfloat16)[:, :48]
        term = jnp.dot(pick, piece, preferred_element_type=jnp.float32)
        total = term if total is None else total + term
    for m in range(4):
        for p in range(3):
            own[m, p] = total[m * 48 : (m + 1) * 48, p * 128 : (p + 1) * 128].astype(jnp.bfloat16)

    def move(m, p, phase, piece, origin, target):
        spots = here.index(m, core, p, phase, origin)
        axis = ORDERS[p][phase]
        src = own.at[m, p] if phase == 0 and origin == 0 else ref_of(spots)
        return pltpu.make_async_remote_copy(
            src_ref=src,
            dst_ref=ref_of(spots),
            send_sem=send.at[m, p, phase, piece],
            recv_sem=recv.at[m, p, phase, piece],
            device_id=here.device(axis, target),
            device_id_type=MESH,
        )

    def arrive(m, p, phase, piece, origin):
        spots = here.index(m, core, p, phase, origin)
        axis = ORDERS[p][phase]
        pltpu.make_async_remote_copy(
            src_ref=ref_of(spots),
            dst_ref=ref_of(spots),
            send_sem=send.at[m, p, phase, piece],
            recv_sem=recv.at[m, p, phase, piece],
            device_id=here.device(axis, 1),
            device_id_type=MESH,
        ).wait_recv()

    def pair(m, p, piece, phase, origin, side):
        spots = here.index(m, side, p, phase, origin)
        return pltpu.make_async_remote_copy(
            src_ref=ref_of(spots),
            dst_ref=ref_of(spots),
            send_sem=pair_send.at[m, p, piece],
            recv_sem=pair_recv.at[m, p, piece],
            device_id=members[0],
            device_id_type=MESH,
        )

    sent = []

    def go(copy):
        copy.start()
        sent.append(copy)

    todo = [(m, p) for m in range(4) for p in range(3)]
    keeps = []
    for m, p in todo:
        go(move(m, p, 0, 0, 0, 1))
        go(move(m, p, 0, 1, 0, 3))
    for m, p in todo:
        copy = pltpu.make_async_copy(own.at[m, p], ref_of(here.index(m, core, p, 0, 0)), keep.at[m, p])
        copy.start()
        keeps.append(copy)
    for copy in keeps:
        copy.wait()
    done = [share]

    def norm_some():
        count = min(share, length // 32 - done[0])
        normalise(done[0], count)
        done[0] += count

    def slide_some(start, count):
        def step(n, _):
            at = pl.ds(pl.multiple_of(n * 128, 128), 128)
            slide_rows[at, :] = project_slide(cache_ref[at, :], slide_gain_ref[...], slide_w_ref)
            return 0

        lax.fori_loop(start, start + count, step, 0)

    slide_copy = pltpu.make_async_copy(slide_rows, slide_ref, slide_store)
    quarter = cache_ref.shape[0] // 128 // 4

    def first_arrivals(m, p, phase):
        arrive(m, p, phase, 0, 3)
        arrive(m, p, phase, 1, 1)
        if m % 2 == 0:
            go(move(m, p, phase, 2, 3, 1))
        else:
            go(move(m, p, phase, 2, 1, 3))
        if phase == 2:
            go(pair(m, p, 1, 2, 3, core))
            go(pair(m, p, 2, 2, 1, core))

    def start_phase(m, p, phase):
        go(move(m, p, phase, 0, 0, 1))
        go(move(m, p, phase, 1, 0, 3))

    def last_arrival(m, p, phase):
        arrive(m, p, phase, 2, 2)
        if phase == 0 or (phase == 1 and m < 2):
            start_phase(m, p, phase + 1)
        if phase == 1:
            go(pair(m, p, 0, 2, 0, core))
        if phase == 2:
            go(pair(m, p, 3, 2, 2, core))

    def from_pair(m, p):
        for piece, origin in enumerate((0, 3, 1, 2)):
            pair(m, p, piece, 2, origin, other).wait_recv()

    def every(step, m, *rest):
        for p in range(3):
            step(m, p, *rest)

    norm_some()
    for phase in range(2):
        for m in range(4):
            every(first_arrivals, m, phase)
        norm_some()
        slide_some(2 * phase * quarter, quarter)
        for m in range(4):
            every(last_arrival, m, phase)
        norm_some()
        slide_some((2 * phase + 1) * quarter, quarter)
    slide_copy.start()
    every(first_arrivals, 0, 2)
    every(start_phase, 2, 2)
    every(last_arrival, 0, 2)
    every(first_arrivals, 1, 2)
    every(start_phase, 3, 2)
    every(from_pair, 0)
    multiply(0, 0, blocks)
    every(last_arrival, 1, 2)
    multiply(0, blocks, blocks)
    every(first_arrivals, 2, 2)
    every(from_pair, 1)
    multiply(1, 0, blocks)
    every(last_arrival, 2, 2)
    multiply(1, blocks, blocks)
    every(first_arrivals, 3, 2)
    every(from_pair, 2)
    multiply(2, 0, blocks)
    every(last_arrival, 3, 2)
    multiply(2, blocks, blocks)
    every(from_pair, 3)
    for slot in range(2):
        store_copy(2, slot, 1, blocks - 2 + slot).wait()
    slide_copy.wait()
    for copy in swaps + sent:
        copy.wait_send()


def project_tiles(tiles, gain, wq, wkv, wo, cache, slide_gain, slide_w):
    rows, width = wq.shape
    slots, length, _ = tiles.shape
    count = slots * length
    parts = jnp.concatenate([wkv, wq, wo], axis=1)
    parts = parts.reshape(rows, 4, 4, width // 4)
    parts = jnp.transpose(parts, (2, 1, 0, 3)).reshape(4, 4 * rows, width // 4)
    dma = pltpu.SemaphoreType.DMA
    hbm = pl.BlockSpec(memory_space=pl.ANY)
    vmem = pl.BlockSpec(memory_space=pltpu.VMEM)
    one = (2, 2, 3, 4, 4, 2, 4 * rows, 128)
    return pl.pallas_call(
        gather_kernel,
        in_specs=[vmem, hbm, vmem, vmem, vmem, vmem],
        out_specs=[hbm, hbm, hbm],
        out_shape=[
            jax.ShapeDtypeStruct((3, width // 128, count, 128), jnp.bfloat16),
            jax.ShapeDtypeStruct(one, jnp.bfloat16),
            jax.ShapeDtypeStruct((cache.shape[0], 3 * 128), jnp.bfloat16),
        ],
        scratch_shapes=[
            pltpu.VMEM((3,) + one, jnp.bfloat16),
            pltpu.VMEM((count, width), jnp.bfloat16),
            pltpu.VMEM((2, 6, ROWS, 128), jnp.bfloat16),
            pltpu.VMEM((3, 4 * rows, width // 4), jnp.bfloat16),
            pltpu.VMEM((4, 3, 4 * rows, 128), jnp.bfloat16),
            pltpu.VMEM((cache.shape[0], 3 * 128), jnp.bfloat16),
            dma((3,)),
            dma((3,)),
            dma((4, 3, 3, 3)),
            dma((4, 3, 3, 3)),
            dma((4, 3, 4)),
            dma((4, 3, 4)),
            dma((4, 3)),
            dma((2,)),
            dma,
            dma,
        ],
        compiler_params=pltpu.CompilerParams(
            collective_id=0, has_side_effects=True, vmem_limit_bytes=48 * 1024 * 1024
        ),
        name="gather_project",
    )(parts, tiles.reshape(count, width), gain, cache, slide_gain, slide_w)


def tile_kernel(
    live_ref, x_ref, gain_ref, kvq, wo_ref, proj_ref, out_ref, fresh_ref,
    wo, proj, emb, ctx, load, proj_load,
):
    step = pl.program_id(0)
    live = live_ref[0]
    tiles, length, width = x_ref.shape
    pairs = width // 128
    load_copy = pltpu.make_async_copy(wo_ref, wo, load)
    proj_copy = pltpu.make_async_copy(proj_ref, proj, proj_load)

    @pl.when(step == 0)
    def _():
        load_copy.start()
        proj_copy.start()

    @pl.when(step * tiles < live)
    def _():
        lane = lax.broadcasted_iota(jnp.int32, (length, 128), 1)
        first = lane < TILE_HEAD_SIZE
        ones_a = jnp.where(first, 1.0, 0.0).astype(jnp.bfloat16)
        ones_b = jnp.where(first, 0.0, 1.0).astype(jnp.bfloat16)
        ones = jnp.concatenate([ones_a, ones_b], axis=0)
        scale = math.log2(math.e) / math.sqrt(TILE_HEAD_SIZE)
        for p in range(pairs):
            for t in range(tiles):
                at = slice(t * length, (t + 1) * length)
                kp, vp, qp = kvq[0, p, at, :], kvq[1, p, at, :], kvq[2, p, at, :]
                keys = jnp.concatenate([kp * ones_a, kp * ones_b], axis=0)
                vals = jnp.concatenate([vp * ones_a, vp * ones_b], axis=0)
                vals = jnp.concatenate([vals, ones], axis=1)
                s = lax.dot_general(
                    qp, keys, (((1,), (1,)), ((), ())), preferred_element_type=jnp.float32
                )
                parts = []
                for half in range(2):
                    sh = s[:, half * length : (half + 1) * length]
                    top = jnp.max(sh, axis=1, keepdims=True)
                    parts.append(jnp.exp2((sh - top) * scale).astype(jnp.bfloat16))
                o = jnp.dot(
                    jnp.concatenate(parts, axis=1), vals, preferred_element_type=jnp.float32
                )
                ctx[p, at, :] = (o[:, :128] / o[:, 128:]).astype(jnp.bfloat16)

    @pl.when(step == 0)
    def _():
        load_copy.wait()

    @pl.when(step * tiles < live)
    def _():
        def project_out(n, _):
            at = pl.ds(pl.multiple_of(n * COLS, COLS), COLS)
            blocks = COLS // 128
            context = jnp.concatenate([ctx[j] for j in range(pairs)], axis=1)
            w = jnp.concatenate([wo[n * blocks + j] for j in range(blocks)], axis=1)
            y = jnp.dot(context, w, preferred_element_type=jnp.float32)
            for t in range(tiles):
                xt = x_ref[t, :, at].astype(jnp.float32)
                yt = xt + y[t * length : (t + 1) * length]
                out_ref[t, :, at] = jnp.where(step * tiles + t < live, yt, 0.0).astype(jnp.bfloat16)
            return 0

        lax.fori_loop(0, width // COLS, project_out, 0)
        for t in range(tiles):
            emb[pl.ds(step * tiles + t, 1), :] = norm_rows(out_ref[t, 0:16, :], gain_ref[1:2, :])[0:1]

    @pl.when(step * tiles >= live)
    def _():
        out_ref[...] = jnp.zeros_like(out_ref)
        for t in range(tiles):
            emb[pl.ds(step * tiles + t, 1), :] = jnp.zeros((1, width), jnp.float32)

    @pl.when(step == pl.num_programs(0) - 1)
    def _():
        proj_copy.wait()
        fresh_ref[...] = jnp.dot(
            emb[...].astype(jnp.bfloat16), proj[...], preferred_element_type=jnp.float32
        ).astype(jnp.bfloat16)


def encode_tiles(live, tiles, gain, kvq, wo, proj):
    slots, length, width = tiles.shape
    rows = GROUP * length
    return pl.pallas_call(
        tile_kernel,
        grid_spec=pltpu.PrefetchScalarGridSpec(
            num_scalar_prefetch=1,
            grid=(slots // GROUP,),
            in_specs=[
                pl.BlockSpec((GROUP, length, width), lambda i, live: (i, 0, 0)),
                pl.BlockSpec(memory_space=pltpu.VMEM),
                pl.BlockSpec((3, width // 128, rows, 128), lambda i, live: (0, 0, i, 0)),
                pl.BlockSpec(memory_space=pl.ANY),
                pl.BlockSpec(memory_space=pl.ANY),
            ],
            out_specs=[
                pl.BlockSpec((GROUP, length, width), lambda i, live: (i, 0, 0)),
                pl.BlockSpec((slots, proj.shape[1]), lambda i, live: (0, 0)),
            ],
            scratch_shapes=[
                pltpu.VMEM((width // 128, width, 128), jnp.bfloat16),
                pltpu.VMEM(proj.shape, jnp.bfloat16),
                pltpu.VMEM((slots, width), jnp.float32),
                pltpu.VMEM((width // 128, rows, 128), jnp.bfloat16),
                pltpu.SemaphoreType.DMA,
                pltpu.SemaphoreType.DMA,
            ],
        ),
        out_shape=[
            jax.ShapeDtypeStruct((slots, length, width), jnp.bfloat16),
            jax.ShapeDtypeStruct((slots, proj.shape[1]), jnp.bfloat16),
        ],
        compiler_params=pltpu.CompilerParams(vmem_limit_bytes=48 * 1024 * 1024),
        name="tile_layer",
    )(live, tiles, gain, kvq, wo, proj)


def slide_kernel(
    fresh_ref, cached_ref, cache_ref, gain_ref, w_ref, live_ref, out_ref,
    fresh, far, qkv, near, fresh_send, fresh_recv, far_send, far_recv, load,
):
    seq, head = lax.axis_index("seq"), lax.axis_index("head")
    groups, slots, width = fresh.shape
    seqs = far.shape[0]
    rows = cached_ref.shape[0]
    span = groups * slots
    load_copy = pltpu.make_async_copy(cached_ref, qkv, load)
    load_copy.start()
    heads = [(seq, (head + j) % groups) for j in range(1, groups)]
    spots = [((seq + j) % seqs, head) for j in range(1, seqs)]
    barrier = pltpu.get_barrier_semaphore()
    for partner in heads + spots:
        pl.semaphore_signal(barrier, inc=1, device_id=partner, device_id_type=MESH)

    fresh[pl.ds(head, 1)] = fresh_ref[...][None]
    pl.semaphore_wait(barrier, len(heads) + len(spots))

    def fresh_copy(j, slot):
        return pltpu.make_async_remote_copy(
            src_ref=fresh.at[slot],
            dst_ref=fresh.at[slot],
            send_sem=fresh_send.at[j],
            recv_sem=fresh_recv.at[j],
            device_id=heads[j],
            device_id_type=MESH,
        )

    def far_copy(j, slot):
        return pltpu.make_async_remote_copy(
            src_ref=far.at[slot],
            dst_ref=far.at[slot],
            send_sem=far_send.at[j],
            recv_sem=far_recv.at[j],
            device_id=spots[j],
            device_id_type=MESH,
        )

    for j in range(groups - 1):
        fresh_copy(j, head).start()

    load_copy.wait()
    for j in range(groups - 1):
        fresh_copy(j, (head + groups - 1 - j) % groups).wait_recv()
    mixed = jnp.where(
        live_ref[...] > 0,
        fresh[...].reshape(span, width).astype(jnp.float32),
        cache_ref[...].astype(jnp.float32),
    )
    qkv[0:span, :] = project_slide(mixed, gain_ref[...], w_ref)

    lane = lax.broadcasted_iota(jnp.int32, (1, 128), 1)
    first = lane < SLIDE_HEAD_SIZE
    thin = rows // RATE
    pick_row = lax.broadcasted_iota(jnp.int32, (2 * thin, rows), 0)
    pick_col = lax.broadcasted_iota(jnp.int32, (2 * thin, rows), 1)
    offset = (2 * head + pick_row // thin) % RATE
    pick = jnp.where(pick_col == (pick_row % thin) * RATE + offset, 1.0, 0.0).astype(jnp.bfloat16)
    sparse = jnp.dot(pick, qkv[...], preferred_element_type=jnp.float32)
    split = lax.broadcasted_iota(jnp.int32, (2 * thin, 128), 0) < thin
    lanes2 = lax.broadcasted_iota(jnp.int32, (2 * thin, 128), 1)
    own_lane = (lanes2 < SLIDE_HEAD_SIZE) == split
    sparse_query = jnp.where(own_lane, sparse[:, :128], 0.0).astype(jnp.bfloat16)
    pairs = []
    for c in (1, 2):
        values = sparse[:, c * 128 : (c + 1) * 128]
        pairs.append(jnp.where(first, values[:thin], values[thin:]))
    far[pl.ds(seq, 1)] = jnp.concatenate(pairs, axis=1).astype(jnp.bfloat16)[None]
    for j in range(seqs - 1):
        far_copy(j, seq).start()

    scale = 1.0 / math.sqrt(SLIDE_HEAD_SIZE)
    ones = jnp.ones((rows, 128), jnp.bfloat16)

    def soften(scores):
        top = jnp.max(scores, axis=1, keepdims=True)
        return jnp.exp((scores - top) * scale).astype(jnp.bfloat16)

    def near_block(n, _):
        at = pl.ds(pl.multiple_of(n * 256, 256), 256)
        parts = []
        values = jnp.concatenate([qkv[:, 256:384], ones], axis=1)
        for side in (first, jnp.logical_not(first)):
            query = qkv[at, 0:128] * jnp.where(side, 1.0, 0.0).astype(jnp.bfloat16)
            scores = lax.dot_general(
                query, qkv[:, 128:256], (((1,), (1,)), ((), ())), preferred_element_type=jnp.float32
            )
            o = jnp.dot(soften(scores), values, preferred_element_type=jnp.float32)
            parts.append(o[:, :128] / o[:, 128:])
        near[at, :] = jnp.where(first, parts[0], parts[1])
        return 0

    lax.fori_loop(0, rows // 256, near_block, 0)

    for j in range(seqs - 1):
        far_copy(j, (seq + seqs - 1 - j) % seqs).wait_recv()
    everyone = far[...].reshape(seqs * thin, 256)
    keys = jnp.concatenate([qkv[:, 128:256], everyone[:, :128]], axis=0)
    values = jnp.concatenate([qkv[:, 256:384], everyone[:, 128:]], axis=0)
    values = jnp.concatenate([values, jnp.ones((rows + seqs * thin, 128), jnp.bfloat16)], axis=1)
    scores = lax.dot_general(
        sparse_query, keys, (((1,), (1,)), ((), ())), preferred_element_type=jnp.float32
    )
    o = jnp.dot(soften(scores), values, preferred_element_type=jnp.float32)
    both = jnp.where(own_lane, o[:, :128] / o[:, 128:], 0.0).astype(jnp.bfloat16)
    place_row = lax.broadcasted_iota(jnp.int32, (rows, 2 * thin), 0)
    place_col = lax.broadcasted_iota(jnp.int32, (rows, 2 * thin), 1)
    offset = (2 * head + place_col // thin) % RATE
    place = jnp.where(place_row == (place_col % thin) * RATE + offset, 1.0, 0.0).astype(jnp.bfloat16)
    spread = jnp.dot(place, both, preferred_element_type=jnp.float32)
    row = lax.broadcasted_iota(jnp.int32, (rows, 128), 0)
    side = lax.broadcasted_iota(jnp.int32, (rows, 128), 1) // SLIDE_HEAD_SIZE
    picked = row % RATE == (2 * head + side) % RATE
    result = jnp.where(picked, spread, near[...]).astype(jnp.bfloat16)
    out_ref[...] = result[:, : out_ref.shape[1]]
    for j in range(groups - 1):
        fresh_copy(j, head).wait_send()
    for j in range(seqs - 1):
        far_copy(j, seq).wait_send()


def encode_slide(fresh, cached, cache, gain, weights, live, groups, seqs):
    slots, width = fresh.shape
    rows, columns = cache.shape[0], weights.shape[2]
    dma = pltpu.SemaphoreType.DMA
    vmem = pl.BlockSpec(memory_space=pltpu.VMEM)
    return pl.pallas_call(
        slide_kernel,
        in_specs=[
            vmem,
            pl.BlockSpec(memory_space=pl.ANY),
            pl.BlockSpec((groups * slots, width), lambda i: (0, 0)),
            vmem,
            vmem,
            vmem,
        ],
        out_specs=vmem,
        grid=(1,),
        out_shape=jax.ShapeDtypeStruct((rows, columns), jnp.bfloat16),
        scratch_shapes=[
            pltpu.VMEM((groups, slots, width), jnp.bfloat16),
            pltpu.VMEM((seqs, rows // RATE, 256), jnp.bfloat16),
            pltpu.VMEM((rows, 3 * 128), jnp.bfloat16),
            pltpu.VMEM((rows, 128), jnp.float32),
            dma((groups - 1,)),
            dma((groups - 1,)),
            dma((seqs - 1,)),
            dma((seqs - 1,)),
            dma,
        ],
        compiler_params=pltpu.CompilerParams(
            collective_id=1, has_side_effects=True, vmem_limit_bytes=48 * 1024 * 1024
        ),
        name="slide_layer",
    )(fresh, cached, cache, gain, weights, live)


def per_device(
    tile_tokens,
    tile_gain,
    tile_wq,
    tile_wkv,
    tile_wo,
    slide_proj,
    slide_cache,
    slide_gain,
    slide_qkv,
    send_map,
):
    local_tiles = tile_tokens[0, 0]
    slot_count = local_tiles.shape[0]
    seq_index = lax.axis_index("seq")
    head_index = lax.axis_index("head")
    kvq, w_out, cached = project_tiles(
        local_tiles, tile_gain, tile_wq, tile_wkv, tile_wo, slide_cache, slide_gain[None], slide_qkv
    )
    w_out = w_out.reshape(kvq.shape[1], -1, 128)
    row_plan = lax.dynamic_index_in_dim(send_map, seq_index, 1, keepdims=False)
    live_count = jnp.sum(row_plan, axis=1)
    own_live = lax.dynamic_slice_in_dim(live_count, head_index, 1, 0)
    tile_layers, fresh = encode_tiles(own_live, local_tiles, tile_gain, kvq, w_out, slide_proj)
    groups, seqs = send_map.shape[0], send_map.shape[1]
    places = jnp.arange(slot_count, dtype=jnp.int32)
    live = (places[None, :] < live_count[:, None]).reshape(groups * slot_count, 1).astype(jnp.float32)
    context = encode_slide(
        fresh, cached, slide_cache, slide_gain[None], slide_qkv, live, groups, seqs
    )
    return (context, tile_layers[None, None])


def solution(mesh):
    return jax.shard_map(
        per_device,
        mesh=mesh,
        in_specs=(
            P("seq", "head", None, None, None),
            P(),
            P(("seq", "head"), None),
            P(("seq", "head"), None),
            P(("seq", "head"), None),
            P(),
            P("seq", None),
            P(),
            P(None, None, "head"),
            P(),
        ),
        out_specs=(P("seq", "head"), P("seq", "head", None, None, None)),
        check_vma=False,
    )
```

```python
import math

import jax
import jax.numpy as jnp
from jax import lax
from jax.experimental import pallas as pl
from jax.experimental.pallas import tpu as pltpu
from jax.sharding import PartitionSpec as P

TILE_HEAD_SIZE = 64
SLIDE_HEAD_SIZE = 48
RATE = 16
EPS = 1e-05
GROUP = 2
COLS = 512
MESH = pl.DeviceIdType.MESH
ORDERS = (("x", "y", "z"), ("y", "z", "x"), ("z", "x", "y"))
RING = 4
ROWS = 1024


def norm_rows(values, gain):
    values = values.astype(jnp.float32)
    center = values - jnp.mean(values, axis=-1, keepdims=True)
    spread = jnp.mean(center * center, axis=-1, keepdims=True)
    return center * lax.rsqrt(spread + EPS) * gain


class Place:
    def __init__(self):
        seq, head = lax.axis_index("seq"), lax.axis_index("head")
        self.core = head % 2
        self.at = {"x": head // 2, "y": seq // RING, "z": seq % RING}

    def device(self, axis=None, shift=0, core=None):
        at = dict(self.at)
        if axis is not None:
            at[axis] = (at[axis] + shift) % RING
        core = self.core if core is None else core
        return (at["y"] * RING + at["z"], at["x"] * 2 + core)

    def index(self, matrix, core, part, phase, shift):
        order = ORDERS[part]
        at = {}
        for number, axis in enumerate(order):
            if number < phase:
                at[axis] = None
            elif number == phase:
                at[axis] = (self.at[axis] + shift) % RING
            else:
                at[axis] = self.at[axis]
        every = slice(None)
        x, y, z = at["x"], at["y"], at["z"]
        low, high = (every, every) if x is None else (x % 2, x // 2)
        return (
            matrix,
            low,
            core,
            part,
            every if y is None else y,
            every if z is None else z,
            high,
        )


def gather_kernel(
    w_ref, x_ref, gain_ref, kvq_ref, last_ref, full, rows_ref, stage, inbox, own,
    swap_send, swap_recv, send, recv, pair_send, pair_recv, keep, store, load,
):
    here = Place()
    length = rows_ref.shape[0]
    load_copy = pltpu.make_async_copy(x_ref, rows_ref, load)
    load_copy.start()

    def normalise(start, count):
        def step(r, _):
            at = pl.ds(pl.multiple_of(r * 64, 64), 64)
            rows_ref[at, :] = norm_rows(rows_ref[at, :], gain_ref[0:1, :]).astype(jnp.bfloat16)
            return 0

        lax.fori_loop(start, start + count, step, 0)

    def ref_of(spots):
        m = spots[0]
        return full.at[spots] if m < 3 else last_ref.at[spots[1:]]

    def store_copy(m, slot, low, block):
        return pltpu.make_async_copy(
            stage.at[slot],
            kvq_ref.at[m, pl.ds(low * 6, 6), pl.ds(pl.multiple_of(block * ROWS, ROWS), ROWS), :],
            store.at[slot],
        )

    blocks = length // ROWS

    def multiply(m, start, count):
        def step(u, _):
            slot, low, block = u % 2, u // blocks, u % blocks

            @pl.when(m * 2 * blocks + u >= 2)
            def _():
                store_copy(m, slot, low, block).wait()

            at = pl.ds(pl.multiple_of(block * ROWS, ROWS), ROWS)
            width = rows_ref.shape[1]
            w = jnp.concatenate(
                [full[m, low, j // 3, j % 3].reshape(width, 128) for j in range(6)], axis=1
            )
            y = jnp.dot(rows_ref[at, :], w, preferred_element_type=jnp.float32).astype(jnp.bfloat16)
            for j in range(6):
                stage[slot, j] = y[:, j * 128 : (j + 1) * 128]
            store_copy(m, slot, low, block).start()
            return 0

        lax.fori_loop(start, start + count, step, 0)
    core, other = here.core, 1 - here.core
    x = here.at["x"]
    low = x % 2
    mate = x + 1 - 2 * low
    spot = here.device()[0]
    members = [(spot, x * 2 + other), (spot, mate * 2 + core), (spot, mate * 2 + other)]
    me = 2 * low + core
    ids = [2 * low + other, 2 * (1 - low) + core, 2 * (1 - low) + other]

    barrier = pltpu.get_barrier_semaphore()
    partners = [here.device(a, s) for a in "xyz" for s in (1, 3)] + [members[0], members[2]]
    for partner in partners:
        pl.semaphore_signal(barrier, inc=1, device_id=partner, device_id_type=MESH)
    pl.semaphore_wait(barrier, len(partners))

    swaps = []
    for n in range(3):
        swaps.append(
            pltpu.make_async_remote_copy(
                src_ref=w_ref.at[ids[n]],
                dst_ref=inbox.at[n],
                send_sem=swap_send.at[n],
                recv_sem=swap_recv.at[n],
                device_id=members[n],
                device_id_type=MESH,
            )
        )
        swaps[n].start()
    share = -(-length // 64 // 5)
    for n in range(3):
        swaps[n].wait_recv()
    count = 4 * 48
    row = lax.broadcasted_iota(jnp.int32, (count, count), 0)
    col = lax.broadcasted_iota(jnp.int32, (count, count), 1)
    matrix, member, inner = row // 48, (row % 48) // 12, row % 12
    total = None
    sources = [w_ref[me]] + [inbox[n] for n in range(3)]
    names = [me] + ids
    for piece, name in zip(sources, names):
        want = matrix * 12 + inner
        pick = jnp.where((member == name) & (want == col), 1.0, 0.0).astype(jnp.bfloat16)[:, :48]
        term = jnp.dot(pick, piece, preferred_element_type=jnp.float32)
        total = term if total is None else total + term
    for m in range(4):
        for p in range(3):
            own[m, p] = total[m * 48 : (m + 1) * 48, p * 128 : (p + 1) * 128].astype(jnp.bfloat16)

    def move(m, p, phase, piece, origin, target):
        spots = here.index(m, core, p, phase, origin)
        axis = ORDERS[p][phase]
        src = own.at[m, p] if phase == 0 and origin == 0 else ref_of(spots)
        return pltpu.make_async_remote_copy(
            src_ref=src,
            dst_ref=ref_of(spots),
            send_sem=send.at[m, p, phase, piece],
            recv_sem=recv.at[m, p, phase, piece],
            device_id=here.device(axis, target),
            device_id_type=MESH,
        )

    def arrive(m, p, phase, piece, origin):
        spots = here.index(m, core, p, phase, origin)
        axis = ORDERS[p][phase]
        pltpu.make_async_remote_copy(
            src_ref=ref_of(spots),
            dst_ref=ref_of(spots),
            send_sem=send.at[m, p, phase, piece],
            recv_sem=recv.at[m, p, phase, piece],
            device_id=here.device(axis, 1),
            device_id_type=MESH,
        ).wait_recv()

    def pair(m, p, piece, phase, origin, side):
        spots = here.index(m, side, p, phase, origin)
        return pltpu.make_async_remote_copy(
            src_ref=ref_of(spots),
            dst_ref=ref_of(spots),
            send_sem=pair_send.at[m, p, piece],
            recv_sem=pair_recv.at[m, p, piece],
            device_id=members[0],
            device_id_type=MESH,
        )

    sent = []

    def go(copy):
        copy.start()
        sent.append(copy)

    todo = [(m, p) for m in range(4) for p in range(3)]
    keeps = []
    for m, p in todo:
        go(move(m, p, 0, 0, 0, 1))
        go(move(m, p, 0, 1, 0, 3))
    for m, p in todo:
        copy = pltpu.make_async_copy(own.at[m, p], ref_of(here.index(m, core, p, 0, 0)), keep.at[m, p])
        copy.start()
        keeps.append(copy)
    for copy in keeps:
        copy.wait()
    done = [0]

    def norm_some():
        count = min(share, length // 64 - done[0])
        normalise(done[0], count)
        done[0] += count

    def first_arrivals(m, p, phase):
        arrive(m, p, phase, 0, 3)
        arrive(m, p, phase, 1, 1)
        if m % 2 == 0:
            go(move(m, p, phase, 2, 3, 1))
        else:
            go(move(m, p, phase, 2, 1, 3))
        if phase == 2:
            go(pair(m, p, 1, 2, 3, core))
            go(pair(m, p, 2, 2, 1, core))

    def start_phase(m, p, phase):
        go(move(m, p, phase, 0, 0, 1))
        go(move(m, p, phase, 1, 0, 3))

    def last_arrival(m, p, phase):
        arrive(m, p, phase, 2, 2)
        if phase == 0 or (phase == 1 and m < 2):
            start_phase(m, p, phase + 1)
        if phase == 1:
            go(pair(m, p, 0, 2, 0, core))
        if phase == 2:
            go(pair(m, p, 3, 2, 2, core))

    def from_pair(m, p):
        for piece, origin in enumerate((0, 3, 1, 2)):
            pair(m, p, piece, 2, origin, other).wait_recv()

    def every(step, m, *rest):
        for p in range(3):
            step(m, p, *rest)

    load_copy.wait()
    norm_some()
    for phase in range(2):
        for m in range(4):
            every(first_arrivals, m, phase)
        norm_some()
        for m in range(4):
            every(last_arrival, m, phase)
        norm_some()
    every(first_arrivals, 0, 2)
    every(start_phase, 2, 2)
    every(last_arrival, 0, 2)
    every(first_arrivals, 1, 2)
    every(start_phase, 3, 2)
    every(from_pair, 0)
    multiply(0, 0, blocks)
    every(last_arrival, 1, 2)
    multiply(0, blocks, blocks)
    every(first_arrivals, 2, 2)
    every(from_pair, 1)
    multiply(1, 0, blocks)
    every(last_arrival, 2, 2)
    multiply(1, blocks, blocks)
    every(first_arrivals, 3, 2)
    every(from_pair, 2)
    multiply(2, 0, blocks)
    every(last_arrival, 3, 2)
    multiply(2, blocks, blocks)
    every(from_pair, 3)
    for slot in range(2):
        store_copy(2, slot, 1, blocks - 2 + slot).wait()
    for copy in swaps + sent:
        copy.wait_send()


def project_tiles(tiles, gain, wq, wkv, wo):
    rows, width = wq.shape
    slots, length, _ = tiles.shape
    count = slots * length
    parts = jnp.concatenate([wkv, wq, wo], axis=1)
    parts = parts.reshape(rows, 4, 4, width // 4)
    parts = jnp.transpose(parts, (2, 1, 0, 3)).reshape(4, 4 * rows, width // 4)
    dma = pltpu.SemaphoreType.DMA
    hbm = pl.BlockSpec(memory_space=pl.ANY)
    vmem = pl.BlockSpec(memory_space=pltpu.VMEM)
    one = (2, 2, 3, 4, 4, 2, 4 * rows, 128)
    return pl.pallas_call(
        gather_kernel,
        in_specs=[vmem, hbm, vmem],
        out_specs=[hbm, hbm],
        out_shape=[
            jax.ShapeDtypeStruct((3, width // 128, count, 128), jnp.bfloat16),
            jax.ShapeDtypeStruct(one, jnp.bfloat16),
        ],
        scratch_shapes=[
            pltpu.VMEM((3,) + one, jnp.bfloat16),
            pltpu.VMEM((count, width), jnp.bfloat16),
            pltpu.VMEM((2, 6, ROWS, 128), jnp.bfloat16),
            pltpu.VMEM((3, 4 * rows, width // 4), jnp.bfloat16),
            pltpu.VMEM((4, 3, 4 * rows, 128), jnp.bfloat16),
            dma((3,)),
            dma((3,)),
            dma((4, 3, 3, 3)),
            dma((4, 3, 3, 3)),
            dma((4, 3, 4)),
            dma((4, 3, 4)),
            dma((4, 3)),
            dma((2,)),
            dma,
        ],
        compiler_params=pltpu.CompilerParams(
            collective_id=0, has_side_effects=True, vmem_limit_bytes=48 * 1024 * 1024
        ),
        name="gather_project",
    )(parts, tiles.reshape(count, width), gain)


def tile_kernel(live_ref, x_ref, gain_ref, kvq, wo_ref, out_ref, emb_ref, wo, ctx, load):
    step = pl.program_id(0)
    live = live_ref[0]
    tiles, length, width = x_ref.shape
    pairs = width // 128
    load_copy = pltpu.make_async_copy(wo_ref, wo, load)

    @pl.when(step == 0)
    def _():
        load_copy.start()

    @pl.when(step * tiles < live)
    def _():
        lane = lax.broadcasted_iota(jnp.int32, (length, 128), 1)
        first = lane < TILE_HEAD_SIZE
        ones_a = jnp.where(first, 1.0, 0.0).astype(jnp.bfloat16)
        ones_b = jnp.where(first, 0.0, 1.0).astype(jnp.bfloat16)
        ones = jnp.concatenate([ones_a, ones_b], axis=0)
        scale = math.log2(math.e) / math.sqrt(TILE_HEAD_SIZE)
        for p in range(pairs):
            for t in range(tiles):
                at = slice(t * length, (t + 1) * length)
                kp, vp, qp = kvq[0, p, at, :], kvq[1, p, at, :], kvq[2, p, at, :]
                keys = jnp.concatenate([kp * ones_a, kp * ones_b], axis=0)
                vals = jnp.concatenate([vp * ones_a, vp * ones_b], axis=0)
                vals = jnp.concatenate([vals, ones], axis=1)
                s = lax.dot_general(
                    qp, keys, (((1,), (1,)), ((), ())), preferred_element_type=jnp.float32
                )
                parts = []
                for half in range(2):
                    sh = s[:, half * length : (half + 1) * length]
                    top = jnp.max(sh, axis=1, keepdims=True)
                    parts.append(jnp.exp2((sh - top) * scale).astype(jnp.bfloat16))
                o = jnp.dot(
                    jnp.concatenate(parts, axis=1), vals, preferred_element_type=jnp.float32
                )
                ctx[p, at, :] = (o[:, :128] / o[:, 128:]).astype(jnp.bfloat16)

    @pl.when(step == 0)
    def _():
        load_copy.wait()

    @pl.when(step * tiles < live)
    def _():
        def project_out(n, _):
            at = pl.ds(pl.multiple_of(n * COLS, COLS), COLS)
            blocks = COLS // 128
            context = jnp.concatenate([ctx[j] for j in range(pairs)], axis=1)
            w = jnp.concatenate([wo[n * blocks + j] for j in range(blocks)], axis=1)
            y = jnp.dot(context, w, preferred_element_type=jnp.float32)
            for t in range(tiles):
                xt = x_ref[t, :, at].astype(jnp.float32)
                yt = xt + y[t * length : (t + 1) * length]
                out_ref[t, :, at] = jnp.where(step * tiles + t < live, yt, 0.0).astype(jnp.bfloat16)
            return 0

        lax.fori_loop(0, width // COLS, project_out, 0)
        for t in range(tiles):
            emb_ref[t] = norm_rows(out_ref[t, 0:16, :], gain_ref[1:2, :])[0:1]

    @pl.when(step * tiles >= live)
    def _():
        out_ref[...] = jnp.zeros_like(out_ref)
        emb_ref[...] = jnp.zeros_like(emb_ref)


def encode_tiles(live, tiles, gain, kvq, wo):
    slots, length, width = tiles.shape
    rows = GROUP * length
    return pl.pallas_call(
        tile_kernel,
        grid_spec=pltpu.PrefetchScalarGridSpec(
            num_scalar_prefetch=1,
            grid=(slots // GROUP,),
            in_specs=[
                pl.BlockSpec((GROUP, length, width), lambda i, live: (i, 0, 0)),
                pl.BlockSpec(memory_space=pltpu.VMEM),
                pl.BlockSpec((3, width // 128, rows, 128), lambda i, live: (0, 0, i, 0)),
                pl.BlockSpec(memory_space=pl.ANY),
            ],
            out_specs=[
                pl.BlockSpec((GROUP, length, width), lambda i, live: (i, 0, 0)),
                pl.BlockSpec((GROUP, 1, width), lambda i, live: (i, 0, 0)),
            ],
            scratch_shapes=[
                pltpu.VMEM((width // 128, width, 128), jnp.bfloat16),
                pltpu.VMEM((width // 128, rows, 128), jnp.bfloat16),
                pltpu.SemaphoreType.DMA,
            ],
        ),
        out_shape=[
            jax.ShapeDtypeStruct((slots, length, width), jnp.bfloat16),
            jax.ShapeDtypeStruct((slots, 1, width), jnp.float32),
        ],
        compiler_params=pltpu.CompilerParams(vmem_limit_bytes=48 * 1024 * 1024),
        name="tile_layer",
    )(live, tiles, gain, kvq, wo)


def slide_kernel(
    emb_ref, proj_ref, cache_ref, gain_ref, w_ref, live_ref, out_ref,
    fresh, far, qkv, near, fresh_send, fresh_recv, far_send, far_recv,
):
    seq, head = lax.axis_index("seq"), lax.axis_index("head")
    groups, slots, width = fresh.shape
    seqs = far.shape[0]
    rows = cache_ref.shape[0]
    span = groups * slots
    heads = [(seq, (head + j) % groups) for j in range(1, groups)]
    spots = [((seq + j) % seqs, head) for j in range(1, seqs)]
    barrier = pltpu.get_barrier_semaphore()
    for partner in heads + spots:
        pl.semaphore_signal(barrier, inc=1, device_id=partner, device_id_type=MESH)

    value = jnp.dot(
        emb_ref[...].astype(jnp.bfloat16), proj_ref[...], preferred_element_type=jnp.float32
    )
    fresh[pl.ds(head, 1)] = value.astype(jnp.bfloat16)[None]
    pl.semaphore_wait(barrier, len(heads) + len(spots))

    def fresh_copy(j, slot):
        return pltpu.make_async_remote_copy(
            src_ref=fresh.at[slot],
            dst_ref=fresh.at[slot],
            send_sem=fresh_send.at[j],
            recv_sem=fresh_recv.at[j],
            device_id=heads[j],
            device_id_type=MESH,
        )

    def far_copy(j, slot):
        return pltpu.make_async_remote_copy(
            src_ref=far.at[slot],
            dst_ref=far.at[slot],
            send_sem=far_send.at[j],
            recv_sem=far_recv.at[j],
            device_id=spots[j],
            device_id_type=MESH,
        )

    for j in range(groups - 1):
        fresh_copy(j, head).start()

    def project(values):
        normed = norm_rows(values, gain_ref[...]).astype(jnp.bfloat16)
        return jnp.dot(normed, w_ref[...], preferred_element_type=jnp.float32).astype(jnp.bfloat16)

    def cached(n, _):
        at = pl.ds(pl.multiple_of(n * 128, 128), 128)
        qkv[at, :] = project(cache_ref[at, :])
        return 0

    lax.fori_loop(span // 128, rows // 128, cached, 0)
    for j in range(groups - 1):
        fresh_copy(j, (head + groups - 1 - j) % groups).wait_recv()
    mixed = jnp.where(
        live_ref[...] > 0,
        fresh[...].reshape(span, width).astype(jnp.float32),
        cache_ref[0:span, :].astype(jnp.float32),
    )
    qkv[0:span, :] = project(mixed)

    lane = lax.broadcasted_iota(jnp.int32, (1, 128), 1)
    first = lane < SLIDE_HEAD_SIZE
    thin = rows // RATE
    pick_row = lax.broadcasted_iota(jnp.int32, (2 * thin, rows), 0)
    pick_col = lax.broadcasted_iota(jnp.int32, (2 * thin, rows), 1)
    offset = (2 * head + pick_row // thin) % RATE
    pick = jnp.where(pick_col == (pick_row % thin) * RATE + offset, 1.0, 0.0).astype(jnp.bfloat16)
    sparse = jnp.dot(pick, qkv[...], preferred_element_type=jnp.float32)
    split = lax.broadcasted_iota(jnp.int32, (2 * thin, 128), 0) < thin
    lanes2 = lax.broadcasted_iota(jnp.int32, (2 * thin, 128), 1)
    own_lane = (lanes2 < SLIDE_HEAD_SIZE) == split
    sparse_query = jnp.where(own_lane, sparse[:, :128], 0.0).astype(jnp.bfloat16)
    pairs = []
    for c in (1, 2):
        values = sparse[:, c * 128 : (c + 1) * 128]
        pairs.append(jnp.where(first, values[:thin], values[thin:]))
    far[pl.ds(seq, 1)] = jnp.concatenate(pairs, axis=1).astype(jnp.bfloat16)[None]
    for j in range(seqs - 1):
        far_copy(j, seq).start()

    scale = 1.0 / math.sqrt(SLIDE_HEAD_SIZE)
    ones = jnp.ones((rows, 128), jnp.bfloat16)

    def soften(scores):
        top = jnp.max(scores, axis=1, keepdims=True)
        return jnp.exp((scores - top) * scale).astype(jnp.bfloat16)

    def near_block(n, _):
        at = pl.ds(pl.multiple_of(n * 256, 256), 256)
        parts = []
        values = jnp.concatenate([qkv[:, 256:384], ones], axis=1)
        for side in (first, jnp.logical_not(first)):
            query = qkv[at, 0:128] * jnp.where(side, 1.0, 0.0).astype(jnp.bfloat16)
            scores = lax.dot_general(
                query, qkv[:, 128:256], (((1,), (1,)), ((), ())), preferred_element_type=jnp.float32
            )
            o = jnp.dot(soften(scores), values, preferred_element_type=jnp.float32)
            parts.append(o[:, :128] / o[:, 128:])
        near[at, :] = jnp.where(first, parts[0], parts[1])
        return 0

    lax.fori_loop(0, rows // 256, near_block, 0)

    for j in range(seqs - 1):
        far_copy(j, (seq + seqs - 1 - j) % seqs).wait_recv()
    everyone = far[...].reshape(seqs * thin, 256)
    keys = jnp.concatenate([qkv[:, 128:256], everyone[:, :128]], axis=0)
    values = jnp.concatenate([qkv[:, 256:384], everyone[:, 128:]], axis=0)
    values = jnp.concatenate([values, jnp.ones((rows + seqs * thin, 128), jnp.bfloat16)], axis=1)
    scores = lax.dot_general(
        sparse_query, keys, (((1,), (1,)), ((), ())), preferred_element_type=jnp.float32
    )
    o = jnp.dot(soften(scores), values, preferred_element_type=jnp.float32)
    both = jnp.where(own_lane, o[:, :128] / o[:, 128:], 0.0).astype(jnp.bfloat16)
    place_row = lax.broadcasted_iota(jnp.int32, (rows, 2 * thin), 0)
    place_col = lax.broadcasted_iota(jnp.int32, (rows, 2 * thin), 1)
    offset = (2 * head + place_col // thin) % RATE
    place = jnp.where(place_row == (place_col % thin) * RATE + offset, 1.0, 0.0).astype(jnp.bfloat16)
    spread = jnp.dot(place, both, preferred_element_type=jnp.float32)
    row = lax.broadcasted_iota(jnp.int32, (rows, 128), 0)
    side = lax.broadcasted_iota(jnp.int32, (rows, 128), 1) // SLIDE_HEAD_SIZE
    picked = row % RATE == (2 * head + side) % RATE
    result = jnp.where(picked, spread, near[...]).astype(jnp.bfloat16)
    out_ref[...] = result[:, : out_ref.shape[1]]
    for j in range(groups - 1):
        fresh_copy(j, head).wait_send()
    for j in range(seqs - 1):
        far_copy(j, seq).wait_send()


def encode_slide(embedded, proj, cache, gain, weights, live, groups, seqs):
    slots, width = embedded.shape[0], proj.shape[1]
    rows, columns = cache.shape[0], weights.shape[2]
    padded = jnp.pad(weights, ((0, 0), (0, 0), (0, 128 - columns)))
    padded = jnp.transpose(padded, (1, 0, 2)).reshape(width, 3 * 128)
    dma = pltpu.SemaphoreType.DMA
    vmem = pl.BlockSpec(memory_space=pltpu.VMEM)
    return pl.pallas_call(
        slide_kernel,
        in_specs=[vmem] * 6,
        out_specs=vmem,
        out_shape=jax.ShapeDtypeStruct((rows, columns), jnp.bfloat16),
        scratch_shapes=[
            pltpu.VMEM((groups, slots, width), jnp.bfloat16),
            pltpu.VMEM((seqs, rows // RATE, 256), jnp.bfloat16),
            pltpu.VMEM((rows, 3 * 128), jnp.bfloat16),
            pltpu.VMEM((rows, 128), jnp.float32),
            dma((groups - 1,)),
            dma((groups - 1,)),
            dma((seqs - 1,)),
            dma((seqs - 1,)),
        ],
        compiler_params=pltpu.CompilerParams(
            collective_id=1, has_side_effects=True, vmem_limit_bytes=48 * 1024 * 1024
        ),
        name="slide_layer",
    )(embedded, proj, cache, gain, padded, live)


def per_device(
    tile_tokens,
    tile_gain,
    tile_wq,
    tile_wkv,
    tile_wo,
    slide_proj,
    slide_cache,
    slide_gain,
    slide_qkv,
    send_map,
):
    local_tiles = tile_tokens[0, 0]
    slot_count = local_tiles.shape[0]
    seq_index = lax.axis_index("seq")
    head_index = lax.axis_index("head")
    kvq, w_out = project_tiles(local_tiles, tile_gain, tile_wq, tile_wkv, tile_wo)
    w_out = w_out.reshape(kvq.shape[1], -1, 128)
    row_plan = lax.dynamic_index_in_dim(send_map, seq_index, 1, keepdims=False)
    live_count = jnp.sum(row_plan, axis=1)
    own_live = lax.dynamic_slice_in_dim(live_count, head_index, 1, 0)
    tile_layers, embedded = encode_tiles(own_live, local_tiles, tile_gain, kvq, w_out)
    groups, seqs = send_map.shape[0], send_map.shape[1]
    places = jnp.arange(slot_count, dtype=jnp.int32)
    live = (places[None, :] < live_count[:, None]).reshape(groups * slot_count, 1).astype(jnp.float32)
    context = encode_slide(
        embedded[:, 0], slide_proj, slide_cache, slide_gain[None], slide_qkv, live, groups, seqs
    )
    return (context, tile_layers[None, None])


def solution(mesh):
    return jax.shard_map(
        per_device,
        mesh=mesh,
        in_specs=(
            P("seq", "head", None, None, None),
            P(),
            P(("seq", "head"), None),
            P(("seq", "head"), None),
            P(("seq", "head"), None),
            P(),
            P("seq", None),
            P(),
            P(None, None, "head"),
            P(),
        ),
        out_specs=(P("seq", "head"), P("seq", "head", None, None, None)),
        check_vma=False,
    )
```

```python
import math

import jax
import jax.numpy as jnp
from jax import lax
from jax.experimental import pallas as pl
from jax.experimental.pallas import tpu as pltpu
from jax.sharding import PartitionSpec as P

TILE_HEAD_SIZE = 64
SLIDE_HEAD_SIZE = 48
RATE = 16
EPS = 1e-05
GROUP = 2
COLS = 512
MESH = pl.DeviceIdType.MESH
ORDERS = (("x", "y", "z"), ("y", "z", "x"), ("z", "x", "y"))
RING = 4
ROWS = 1024


def norm_rows(values, gain):
    values = values.astype(jnp.float32)
    center = values - jnp.mean(values, axis=-1, keepdims=True)
    spread = jnp.mean(center * center, axis=-1, keepdims=True)
    return center * lax.rsqrt(spread + EPS) * gain


class Place:
    def __init__(self):
        seq, head = lax.axis_index("seq"), lax.axis_index("head")
        self.core = head % 2
        self.at = {"x": head // 2, "y": seq // RING, "z": seq % RING}

    def device(self, axis=None, shift=0, core=None):
        at = dict(self.at)
        if axis is not None:
            at[axis] = (at[axis] + shift) % RING
        core = self.core if core is None else core
        return (at["y"] * RING + at["z"], at["x"] * 2 + core)

    def index(self, matrix, core, part, phase, shift):
        order = ORDERS[part]
        at = {}
        for number, axis in enumerate(order):
            if number < phase:
                at[axis] = None
            elif number == phase:
                at[axis] = (self.at[axis] + shift) % RING
            else:
                at[axis] = self.at[axis]
        every = slice(None)
        x, y, z = at["x"], at["y"], at["z"]
        low, high = (every, every) if x is None else (x % 2, x // 2)
        return (
            matrix,
            low,
            core,
            part,
            every if y is None else y,
            every if z is None else z,
            high,
        )


def gather_kernel(
    w_ref, x_ref, gain_ref, kvq_ref, last_ref, full, rows_ref, stage, inbox, own,
    swap_send, swap_recv, send, recv, pair_send, pair_recv, keep, store, load,
):
    here = Place()
    length = rows_ref.shape[0]
    load_copy = pltpu.make_async_copy(x_ref, rows_ref, load)
    load_copy.start()

    def normalise(start, count):
        def step(r, _):
            at = pl.ds(pl.multiple_of(r * 64, 64), 64)
            rows_ref[at, :] = norm_rows(rows_ref[at, :], gain_ref[0:1, :]).astype(jnp.bfloat16)
            return 0

        lax.fori_loop(start, start + count, step, 0)

    def ref_of(spots):
        m = spots[0]
        return full.at[spots] if m < 3 else last_ref.at[spots[1:]]

    def store_copy(m, slot, low, block):
        return pltpu.make_async_copy(
            stage.at[slot],
            kvq_ref.at[m, pl.ds(low * 6, 6), pl.ds(pl.multiple_of(block * ROWS, ROWS), ROWS), :],
            store.at[slot],
        )

    blocks = length // ROWS

    def multiply(m, start, count):
        def step(u, _):
            slot, low, block = u % 2, u // blocks, u % blocks

            @pl.when(m * 2 * blocks + u >= 2)
            def _():
                store_copy(m, slot, low, block).wait()

            at = pl.ds(pl.multiple_of(block * ROWS, ROWS), ROWS)
            width = rows_ref.shape[1]
            w = jnp.concatenate(
                [full[m, low, j // 3, j % 3].reshape(width, 128) for j in range(6)], axis=1
            )
            y = jnp.dot(rows_ref[at, :], w, preferred_element_type=jnp.float32).astype(jnp.bfloat16)
            for j in range(6):
                stage[slot, j] = y[:, j * 128 : (j + 1) * 128]
            store_copy(m, slot, low, block).start()
            return 0

        lax.fori_loop(start, start + count, step, 0)
    core, other = here.core, 1 - here.core
    x = here.at["x"]
    low = x % 2
    mate = x + 1 - 2 * low
    spot = here.device()[0]
    members = [(spot, x * 2 + other), (spot, mate * 2 + core), (spot, mate * 2 + other)]
    me = 2 * low + core
    ids = [2 * low + other, 2 * (1 - low) + core, 2 * (1 - low) + other]

    barrier = pltpu.get_barrier_semaphore()
    partners = [here.device(a, s) for a in "xyz" for s in (1, 3)] + [members[0], members[2]]
    for partner in partners:
        pl.semaphore_signal(barrier, inc=1, device_id=partner, device_id_type=MESH)
    pl.semaphore_wait(barrier, len(partners))

    swaps = []
    for n in range(3):
        swaps.append(
            pltpu.make_async_remote_copy(
                src_ref=w_ref.at[ids[n]],
                dst_ref=inbox.at[n],
                send_sem=swap_send.at[n],
                recv_sem=swap_recv.at[n],
                device_id=members[n],
                device_id_type=MESH,
            )
        )
        swaps[n].start()
    share = -(-length // 64 // 5)
    for n in range(3):
        swaps[n].wait_recv()
    count = 4 * 48
    row = lax.broadcasted_iota(jnp.int32, (count, count), 0)
    col = lax.broadcasted_iota(jnp.int32, (count, count), 1)
    matrix, member, inner = row // 48, (row % 48) // 12, row % 12
    total = None
    sources = [w_ref[me]] + [inbox[n] for n in range(3)]
    names = [me] + ids
    for piece, name in zip(sources, names):
        want = matrix * 12 + inner
        pick = jnp.where((member == name) & (want == col), 1.0, 0.0).astype(jnp.bfloat16)[:, :48]
        term = jnp.dot(pick, piece, preferred_element_type=jnp.float32)
        total = term if total is None else total + term
    for m in range(4):
        for p in range(3):
            own[m, p] = total[m * 48 : (m + 1) * 48, p * 128 : (p + 1) * 128].astype(jnp.bfloat16)

    def move(m, p, phase, piece, origin, target):
        spots = here.index(m, core, p, phase, origin)
        axis = ORDERS[p][phase]
        src = own.at[m, p] if phase == 0 and origin == 0 else ref_of(spots)
        return pltpu.make_async_remote_copy(
            src_ref=src,
            dst_ref=ref_of(spots),
            send_sem=send.at[m, p, phase, piece],
            recv_sem=recv.at[m, p, phase, piece],
            device_id=here.device(axis, target),
            device_id_type=MESH,
        )

    def arrive(m, p, phase, piece, origin):
        spots = here.index(m, core, p, phase, origin)
        axis = ORDERS[p][phase]
        pltpu.make_async_remote_copy(
            src_ref=ref_of(spots),
            dst_ref=ref_of(spots),
            send_sem=send.at[m, p, phase, piece],
            recv_sem=recv.at[m, p, phase, piece],
            device_id=here.device(axis, 1),
            device_id_type=MESH,
        ).wait_recv()

    def pair(m, p, piece, phase, origin, side):
        spots = here.index(m, side, p, phase, origin)
        return pltpu.make_async_remote_copy(
            src_ref=ref_of(spots),
            dst_ref=ref_of(spots),
            send_sem=pair_send.at[m, p, piece],
            recv_sem=pair_recv.at[m, p, piece],
            device_id=members[0],
            device_id_type=MESH,
        )

    sent = []

    def go(copy):
        copy.start()
        sent.append(copy)

    todo = [(m, p) for m in range(4) for p in range(3)]
    keeps = []
    for m, p in todo:
        go(move(m, p, 0, 0, 0, 1))
        go(move(m, p, 0, 1, 0, 3))
    for m, p in todo:
        copy = pltpu.make_async_copy(own.at[m, p], ref_of(here.index(m, core, p, 0, 0)), keep.at[m, p])
        copy.start()
        keeps.append(copy)
    for copy in keeps:
        copy.wait()
    done = [0]

    def norm_some():
        count = min(share, length // 64 - done[0])
        normalise(done[0], count)
        done[0] += count

    def first_arrivals(m, p, phase):
        arrive(m, p, phase, 0, 3)
        arrive(m, p, phase, 1, 1)
        if m % 2 == 0:
            go(move(m, p, phase, 2, 3, 1))
        else:
            go(move(m, p, phase, 2, 1, 3))
        if phase == 2:
            go(pair(m, p, 1, 2, 3, core))
            go(pair(m, p, 2, 2, 1, core))

    def start_phase(m, p, phase):
        go(move(m, p, phase, 0, 0, 1))
        go(move(m, p, phase, 1, 0, 3))

    def last_arrival(m, p, phase):
        arrive(m, p, phase, 2, 2)
        if phase == 0 or (phase == 1 and m < 2):
            start_phase(m, p, phase + 1)
        if phase == 1:
            go(pair(m, p, 0, 2, 0, core))
        if phase == 2:
            go(pair(m, p, 3, 2, 2, core))

    def from_pair(m, p):
        for piece, origin in enumerate((0, 3, 1, 2)):
            pair(m, p, piece, 2, origin, other).wait_recv()

    def every(step, m, *rest):
        for p in range(3):
            step(m, p, *rest)

    load_copy.wait()
    norm_some()
    for phase in range(2):
        for m in range(4):
            every(first_arrivals, m, phase)
        norm_some()
        for m in range(4):
            every(last_arrival, m, phase)
        norm_some()
    every(first_arrivals, 0, 2)
    every(start_phase, 2, 2)
    every(first_arrivals, 1, 2)
    every(start_phase, 3, 2)
    every(last_arrival, 0, 2)
    every(from_pair, 0)
    multiply(0, 0, blocks)
    every(last_arrival, 1, 2)
    multiply(0, blocks, blocks)
    every(first_arrivals, 2, 2)
    every(from_pair, 1)
    multiply(1, 0, blocks)
    every(last_arrival, 2, 2)
    multiply(1, blocks, blocks)
    every(first_arrivals, 3, 2)
    every(from_pair, 2)
    multiply(2, 0, blocks)
    every(last_arrival, 3, 2)
    multiply(2, blocks, blocks)
    every(from_pair, 3)
    for slot in range(2):
        store_copy(2, slot, 1, blocks - 2 + slot).wait()
    for copy in swaps + sent:
        copy.wait_send()


def project_tiles(tiles, gain, wq, wkv, wo):
    rows, width = wq.shape
    slots, length, _ = tiles.shape
    count = slots * length
    parts = jnp.concatenate([wkv, wq, wo], axis=1)
    parts = parts.reshape(rows, 4, 4, width // 4)
    parts = jnp.transpose(parts, (2, 1, 0, 3)).reshape(4, 4 * rows, width // 4)
    dma = pltpu.SemaphoreType.DMA
    hbm = pl.BlockSpec(memory_space=pl.ANY)
    vmem = pl.BlockSpec(memory_space=pltpu.VMEM)
    one = (2, 2, 3, 4, 4, 2, 4 * rows, 128)
    return pl.pallas_call(
        gather_kernel,
        in_specs=[vmem, hbm, vmem],
        out_specs=[hbm, hbm],
        out_shape=[
            jax.ShapeDtypeStruct((3, width // 128, count, 128), jnp.bfloat16),
            jax.ShapeDtypeStruct(one, jnp.bfloat16),
        ],
        scratch_shapes=[
            pltpu.VMEM((3,) + one, jnp.bfloat16),
            pltpu.VMEM((count, width), jnp.bfloat16),
            pltpu.VMEM((2, 6, ROWS, 128), jnp.bfloat16),
            pltpu.VMEM((3, 4 * rows, width // 4), jnp.bfloat16),
            pltpu.VMEM((4, 3, 4 * rows, 128), jnp.bfloat16),
            dma((3,)),
            dma((3,)),
            dma((4, 3, 3, 3)),
            dma((4, 3, 3, 3)),
            dma((4, 3, 4)),
            dma((4, 3, 4)),
            dma((4, 3)),
            dma((2,)),
            dma,
        ],
        compiler_params=pltpu.CompilerParams(
            collective_id=0, has_side_effects=True, vmem_limit_bytes=48 * 1024 * 1024
        ),
        name="gather_project",
    )(parts, tiles.reshape(count, width), gain)


def tile_kernel(live_ref, x_ref, gain_ref, kvq, wo_ref, out_ref, emb_ref, wo, ctx, load):
    step = pl.program_id(0)
    live = live_ref[0]
    tiles, length, width = x_ref.shape
    pairs = width // 128
    load_copy = pltpu.make_async_copy(wo_ref, wo, load)

    @pl.when(step == 0)
    def _():
        load_copy.start()

    @pl.when(step * tiles < live)
    def _():
        lane = lax.broadcasted_iota(jnp.int32, (length, 128), 1)
        first = lane < TILE_HEAD_SIZE
        ones_a = jnp.where(first, 1.0, 0.0).astype(jnp.bfloat16)
        ones_b = jnp.where(first, 0.0, 1.0).astype(jnp.bfloat16)
        ones = jnp.concatenate([ones_a, ones_b], axis=0)
        scale = math.log2(math.e) / math.sqrt(TILE_HEAD_SIZE)
        for p in range(pairs):
            for t in range(tiles):
                at = slice(t * length, (t + 1) * length)
                kp, vp, qp = kvq[0, p, at, :], kvq[1, p, at, :], kvq[2, p, at, :]
                keys = jnp.concatenate([kp * ones_a, kp * ones_b], axis=0)
                vals = jnp.concatenate([vp * ones_a, vp * ones_b], axis=0)
                vals = jnp.concatenate([vals, ones], axis=1)
                s = lax.dot_general(
                    qp, keys, (((1,), (1,)), ((), ())), preferred_element_type=jnp.float32
                )
                parts = []
                for half in range(2):
                    sh = s[:, half * length : (half + 1) * length]
                    top = jnp.max(sh, axis=1, keepdims=True)
                    parts.append(jnp.exp2((sh - top) * scale).astype(jnp.bfloat16))
                o = jnp.dot(
                    jnp.concatenate(parts, axis=1), vals, preferred_element_type=jnp.float32
                )
                ctx[p, at, :] = (o[:, :128] / o[:, 128:]).astype(jnp.bfloat16)

    @pl.when(step == 0)
    def _():
        load_copy.wait()

    @pl.when(step * tiles < live)
    def _():
        def project_out(n, _):
            at = pl.ds(pl.multiple_of(n * COLS, COLS), COLS)
            blocks = COLS // 128
            context = jnp.concatenate([ctx[j] for j in range(pairs)], axis=1)
            w = jnp.concatenate([wo[n * blocks + j] for j in range(blocks)], axis=1)
            y = jnp.dot(context, w, preferred_element_type=jnp.float32)
            for t in range(tiles):
                xt = x_ref[t, :, at].astype(jnp.float32)
                yt = xt + y[t * length : (t + 1) * length]
                out_ref[t, :, at] = jnp.where(step * tiles + t < live, yt, 0.0).astype(jnp.bfloat16)
            return 0

        lax.fori_loop(0, width // COLS, project_out, 0)
        for t in range(tiles):
            emb_ref[t] = norm_rows(out_ref[t, 0:16, :], gain_ref[1:2, :])[0:1]

    @pl.when(step * tiles >= live)
    def _():
        out_ref[...] = jnp.zeros_like(out_ref)
        emb_ref[...] = jnp.zeros_like(emb_ref)


def encode_tiles(live, tiles, gain, kvq, wo):
    slots, length, width = tiles.shape
    rows = GROUP * length
    return pl.pallas_call(
        tile_kernel,
        grid_spec=pltpu.PrefetchScalarGridSpec(
            num_scalar_prefetch=1,
            grid=(slots // GROUP,),
            in_specs=[
                pl.BlockSpec((GROUP, length, width), lambda i, live: (i, 0, 0)),
                pl.BlockSpec(memory_space=pltpu.VMEM),
                pl.BlockSpec((3, width // 128, rows, 128), lambda i, live: (0, 0, i, 0)),
                pl.BlockSpec(memory_space=pl.ANY),
            ],
            out_specs=[
                pl.BlockSpec((GROUP, length, width), lambda i, live: (i, 0, 0)),
                pl.BlockSpec((GROUP, 1, width), lambda i, live: (i, 0, 0)),
            ],
            scratch_shapes=[
                pltpu.VMEM((width // 128, width, 128), jnp.bfloat16),
                pltpu.VMEM((width // 128, rows, 128), jnp.bfloat16),
                pltpu.SemaphoreType.DMA,
            ],
        ),
        out_shape=[
            jax.ShapeDtypeStruct((slots, length, width), jnp.bfloat16),
            jax.ShapeDtypeStruct((slots, 1, width), jnp.float32),
        ],
        compiler_params=pltpu.CompilerParams(vmem_limit_bytes=48 * 1024 * 1024),
        name="tile_layer",
    )(live, tiles, gain, kvq, wo)


def slide_kernel(
    emb_ref, proj_ref, cache_ref, gain_ref, w_ref, live_ref, out_ref,
    fresh, far, qkv, near, fresh_send, fresh_recv, far_send, far_recv,
):
    seq, head = lax.axis_index("seq"), lax.axis_index("head")
    groups, slots, width = fresh.shape
    seqs = far.shape[0]
    rows = cache_ref.shape[0]
    span = groups * slots
    heads = [(seq, (head + j) % groups) for j in range(1, groups)]
    spots = [((seq + j) % seqs, head) for j in range(1, seqs)]
    barrier = pltpu.get_barrier_semaphore()
    for partner in heads + spots:
        pl.semaphore_signal(barrier, inc=1, device_id=partner, device_id_type=MESH)

    value = jnp.dot(
        emb_ref[...].astype(jnp.bfloat16), proj_ref[...], preferred_element_type=jnp.float32
    )
    fresh[pl.ds(head, 1)] = value.astype(jnp.bfloat16)[None]
    pl.semaphore_wait(barrier, len(heads) + len(spots))

    def fresh_copy(j, slot):
        return pltpu.make_async_remote_copy(
            src_ref=fresh.at[slot],
            dst_ref=fresh.at[slot],
            send_sem=fresh_send.at[j],
            recv_sem=fresh_recv.at[j],
            device_id=heads[j],
            device_id_type=MESH,
        )

    def far_copy(j, slot):
        return pltpu.make_async_remote_copy(
            src_ref=far.at[slot],
            dst_ref=far.at[slot],
            send_sem=far_send.at[j],
            recv_sem=far_recv.at[j],
            device_id=spots[j],
            device_id_type=MESH,
        )

    for j in range(groups - 1):
        fresh_copy(j, head).start()

    def project(values):
        normed = norm_rows(values, gain_ref[...]).astype(jnp.bfloat16)
        return jnp.dot(normed, w_ref[...], preferred_element_type=jnp.float32).astype(jnp.bfloat16)

    def cached(n, _):
        at = pl.ds(pl.multiple_of(n * 128, 128), 128)
        qkv[at, :] = project(cache_ref[at, :])
        return 0

    lax.fori_loop(span // 128, rows // 128, cached, 0)
    for j in range(groups - 1):
        fresh_copy(j, (head + groups - 1 - j) % groups).wait_recv()
    mixed = jnp.where(
        live_ref[...] > 0,
        fresh[...].reshape(span, width).astype(jnp.float32),
        cache_ref[0:span, :].astype(jnp.float32),
    )
    qkv[0:span, :] = project(mixed)

    lane = lax.broadcasted_iota(jnp.int32, (1, 128), 1)
    first = lane < SLIDE_HEAD_SIZE
    thin = rows // RATE
    pick_row = lax.broadcasted_iota(jnp.int32, (2 * thin, rows), 0)
    pick_col = lax.broadcasted_iota(jnp.int32, (2 * thin, rows), 1)
    offset = (2 * head + pick_row // thin) % RATE
    pick = jnp.where(pick_col == (pick_row % thin) * RATE + offset, 1.0, 0.0).astype(jnp.bfloat16)
    sparse = jnp.dot(pick, qkv[...], preferred_element_type=jnp.float32)
    split = lax.broadcasted_iota(jnp.int32, (2 * thin, 128), 0) < thin
    lanes2 = lax.broadcasted_iota(jnp.int32, (2 * thin, 128), 1)
    own_lane = (lanes2 < SLIDE_HEAD_SIZE) == split
    sparse_query = jnp.where(own_lane, sparse[:, :128], 0.0).astype(jnp.bfloat16)
    pairs = []
    for c in (1, 2):
        values = sparse[:, c * 128 : (c + 1) * 128]
        pairs.append(jnp.where(first, values[:thin], values[thin:]))
    far[pl.ds(seq, 1)] = jnp.concatenate(pairs, axis=1).astype(jnp.bfloat16)[None]
    for j in range(seqs - 1):
        far_copy(j, seq).start()

    scale = 1.0 / math.sqrt(SLIDE_HEAD_SIZE)
    ones = jnp.ones((rows, 128), jnp.bfloat16)

    def soften(scores):
        top = jnp.max(scores, axis=1, keepdims=True)
        return jnp.exp((scores - top) * scale).astype(jnp.bfloat16)

    def near_block(n, _):
        at = pl.ds(pl.multiple_of(n * 256, 256), 256)
        parts = []
        values = jnp.concatenate([qkv[:, 256:384], ones], axis=1)
        for side in (first, jnp.logical_not(first)):
            query = qkv[at, 0:128] * jnp.where(side, 1.0, 0.0).astype(jnp.bfloat16)
            scores = lax.dot_general(
                query, qkv[:, 128:256], (((1,), (1,)), ((), ())), preferred_element_type=jnp.float32
            )
            o = jnp.dot(soften(scores), values, preferred_element_type=jnp.float32)
            parts.append(o[:, :128] / o[:, 128:])
        near[at, :] = jnp.where(first, parts[0], parts[1])
        return 0

    lax.fori_loop(0, rows // 256, near_block, 0)

    for j in range(seqs - 1):
        far_copy(j, (seq + seqs - 1 - j) % seqs).wait_recv()
    everyone = far[...].reshape(seqs * thin, 256)
    keys = jnp.concatenate([qkv[:, 128:256], everyone[:, :128]], axis=0)
    values = jnp.concatenate([qkv[:, 256:384], everyone[:, 128:]], axis=0)
    values = jnp.concatenate([values, jnp.ones((rows + seqs * thin, 128), jnp.bfloat16)], axis=1)
    scores = lax.dot_general(
        sparse_query, keys, (((1,), (1,)), ((), ())), preferred_element_type=jnp.float32
    )
    o = jnp.dot(soften(scores), values, preferred_element_type=jnp.float32)
    both = jnp.where(own_lane, o[:, :128] / o[:, 128:], 0.0).astype(jnp.bfloat16)
    place_row = lax.broadcasted_iota(jnp.int32, (rows, 2 * thin), 0)
    place_col = lax.broadcasted_iota(jnp.int32, (rows, 2 * thin), 1)
    offset = (2 * head + place_col // thin) % RATE
    place = jnp.where(place_row == (place_col % thin) * RATE + offset, 1.0, 0.0).astype(jnp.bfloat16)
    spread = jnp.dot(place, both, preferred_element_type=jnp.float32)
    row = lax.broadcasted_iota(jnp.int32, (rows, 128), 0)
    side = lax.broadcasted_iota(jnp.int32, (rows, 128), 1) // SLIDE_HEAD_SIZE
    picked = row % RATE == (2 * head + side) % RATE
    result = jnp.where(picked, spread, near[...]).astype(jnp.bfloat16)
    out_ref[...] = result[:, : out_ref.shape[1]]
    for j in range(groups - 1):
        fresh_copy(j, head).wait_send()
    for j in range(seqs - 1):
        far_copy(j, seq).wait_send()


def encode_slide(embedded, proj, cache, gain, weights, live, groups, seqs):
    slots, width = embedded.shape[0], proj.shape[1]
    rows, columns = cache.shape[0], weights.shape[2]
    padded = jnp.pad(weights, ((0, 0), (0, 0), (0, 128 - columns)))
    padded = jnp.transpose(padded, (1, 0, 2)).reshape(width, 3 * 128)
    dma = pltpu.SemaphoreType.DMA
    vmem = pl.BlockSpec(memory_space=pltpu.VMEM)
    return pl.pallas_call(
        slide_kernel,
        in_specs=[vmem] * 6,
        out_specs=vmem,
        out_shape=jax.ShapeDtypeStruct((rows, columns), jnp.bfloat16),
        scratch_shapes=[
            pltpu.VMEM((groups, slots, width), jnp.bfloat16),
            pltpu.VMEM((seqs, rows // RATE, 256), jnp.bfloat16),
            pltpu.VMEM((rows, 3 * 128), jnp.bfloat16),
            pltpu.VMEM((rows, 128), jnp.float32),
            dma((groups - 1,)),
            dma((groups - 1,)),
            dma((seqs - 1,)),
            dma((seqs - 1,)),
        ],
        compiler_params=pltpu.CompilerParams(
            collective_id=1, has_side_effects=True, vmem_limit_bytes=48 * 1024 * 1024
        ),
        name="slide_layer",
    )(embedded, proj, cache, gain, padded, live)


def per_device(
    tile_tokens,
    tile_gain,
    tile_wq,
    tile_wkv,
    tile_wo,
    slide_proj,
    slide_cache,
    slide_gain,
    slide_qkv,
    send_map,
):
    local_tiles = tile_tokens[0, 0]
    slot_count = local_tiles.shape[0]
    seq_index = lax.axis_index("seq")
    head_index = lax.axis_index("head")
    kvq, w_out = project_tiles(local_tiles, tile_gain, tile_wq, tile_wkv, tile_wo)
    w_out = w_out.reshape(kvq.shape[1], -1, 128)
    row_plan = lax.dynamic_index_in_dim(send_map, seq_index, 1, keepdims=False)
    live_count = jnp.sum(row_plan, axis=1)
    own_live = lax.dynamic_slice_in_dim(live_count, head_index, 1, 0)
    tile_layers, embedded = encode_tiles(own_live, local_tiles, tile_gain, kvq, w_out)
    groups, seqs = send_map.shape[0], send_map.shape[1]
    places = jnp.arange(slot_count, dtype=jnp.int32)
    live = (places[None, :] < live_count[:, None]).reshape(groups * slot_count, 1).astype(jnp.float32)
    context = encode_slide(
        embedded[:, 0], slide_proj, slide_cache, slide_gain[None], slide_qkv, live, groups, seqs
    )
    return (context, tile_layers[None, None])


def solution(mesh):
    return jax.shard_map(
        per_device,
        mesh=mesh,
        in_specs=(
            P("seq", "head", None, None, None),
            P(),
            P(("seq", "head"), None),
            P(("seq", "head"), None),
            P(("seq", "head"), None),
            P(),
            P("seq", None),
            P(),
            P(None, None, "head"),
            P(),
        ),
        out_specs=(P("seq", "head"), P("seq", "head", None, None, None)),
        check_vma=False,
    )
```
